128 devices in a mesh: dp: 128 (over x, y, z, core).
Axes of the slice: x: 4, y: 4, z: 4, core: 2. Of those that a mesh axis runs over, the one named last changes fastest.
Arguments:
- grad_query: bfloat16 [128, 64, 8192], P('dp'), may hold values from -6 to 6
- grad_gate: bfloat16 [128, 128, 8192], P('dp'), may hold values from -24 to 24
- old_master: float32 [2883584], P('dp'), may hold values from -6 to 6
- old_moment: float32 [2883584], P('dp'), may hold values from -6 to 6
- old_variance: float32 [2883584], P('dp'), may hold values from 0.5 to 8
- old_bounds: int32 [128, 2], P('dp'), may hold values from 0 to 1572864, as said below
Outputs:
- new_master: float32 [1572864], P('dp')
- new_moment: float32 [1572864], P('dp')
- new_variance: float32 [1572864], P('dp')
- query_weight: bfloat16 [64, 8192], replicated
- gate_weight: bfloat16 [128, 8192], replicated
The draws below stay inside these ranges and needn't reach their ends.
Inputs may be any that keep to these rules, and one draw needn't show every extreme that they name: `old_bounds`: the 96 old buckets, in the order of old owners, tile 0 to 1572864: old owner i's bucket stands in row 4 (i // 3) + i % 3, and the last ends at 1572864. Old owner 3k starts exactly at 4 k * 12288; every other start lies on a multiple of 128 within 3072 of i * 16384. A row whose index is 3 mod 4 holds an empty bucket, both entries equal to the end of the row before it. One bucket has exactly 22528 positions.
All inputs are finite; a program needn't handle non-finite values.
Results may differ from the reference program's by a relative error of at most 0.001.
Values may be sent and summed in bfloat16 or wider, within the bound.
A program may use at most 64 MiB of HBM per device.

```python
import math
import jax
import jax.numpy as jnp
from jax import lax

D = 8192
QROWS = 64
GROWS = 128
STEP = 10
ALIGN = 128
PARAMS = 1572864
OLD = 96
OSHARD = 16384
REACH = 3072
BUCKET = 22528
N_DP = 128


def draw_old_bounds(key, part):
    key = jax.random.fold_in(key, 7)
    key_jitter, key_chosen = jax.random.split(key)
    reach_steps = REACH // ALIGN
    jitter = jax.random.randint(key_jitter, (OLD,), -reach_steps, reach_steps + 1) * ALIGN
    owners = jnp.arange(OLD)
    jitter = jnp.where(owners % 3 == 0, 0, jitter)
    chosen = 3 * jax.random.randint(key_chosen, (), 0, OLD // 3) + 1
    jitter = jnp.where(owners == chosen, -REACH, jitter)
    jitter = jnp.where(owners == chosen + 1, REACH, jitter)
    starts = owners * OSHARD + jitter
    finish = jnp.concatenate([starts[1:], jnp.array([PARAMS])])
    old_rows = jnp.stack([starts, finish], axis=1).reshape(N_DP // 4, 3, 2)
    ends = old_rows[:, 2, 1]
    empty_rows = jnp.stack([ends, ends], axis=1)[:, None, :]
    return jnp.concatenate([old_rows, empty_rows], axis=1).reshape(N_DP, 2).astype(jnp.int32)


def raised(result, own_key, source, target, blocks, factor):
    def block_of(axis_at):
        return (jnp.arange(result.shape[axis_at]) // (result.shape[axis_at] // blocks)).reshape((-1,) + (1,) * (result.ndim - 1 - axis_at))

    one_side = jax.random.permutation(own_key, blocks)[block_of(target)]
    far = (block_of(target) + blocks // 2) % blocks
    return jnp.where((block_of(source) == one_side) | (block_of(source) == far), factor * result, result)


def shard_levels(rng, extent, cuts, low, high):
    factor_of = 1.0
    for position, blocks in cuts:
        heights = jax.random.uniform(jax.random.fold_in(jax.random.fold_in(rng, 6), position), (blocks,), jnp.float32, low / len(cuts), high / len(cuts))
        factor_of = factor_of * jnp.repeat(jnp.exp(heights), extent[position] // blocks).reshape((-1,) + (1,) * (len(extent) - 1 - position))
    return factor_of


def scatter_about(key, extent, width, reach, shards=(), kind=jnp.bfloat16):
    factor_of = shard_levels(key, extent, shards, -0.22, 0.18) if shards else 1.0
    entries = jax.random.normal(key, extent, jnp.float32) * width * factor_of
    return jnp.minimum(jnp.maximum(entries, -reach), reach).astype(kind)


def heavy_noise(stream_key, dims, spread, most, cuts, heavy, dtype=jnp.bfloat16):
    result = spread * jax.random.normal(stream_key, dims, jnp.float32)
    if cuts:
        result = result * shard_levels(stream_key, dims, cuts, -0.22, 0.18)
    return jnp.clip(raised(result, jax.random.fold_in(stream_key, 3), *heavy), -most, most).astype(dtype)


def setup_inputs(seed: int = 0) -> dict:
    key_of = jax.random.split(jax.random.key(seed), 7)
    grad_query = scatter_about(key_of[0], (N_DP, QROWS, D), 1.0, 6.0, ((0, 128),))
    grad_gate = heavy_noise(key_of[1], (N_DP, GROWS, D), 1.0, 24.0, ((0, 128),), (0, 1, 128, 5.5))
    old_master = scatter_about(key_of[2], (N_DP * BUCKET,), 1.0, 6.0, ((0, 128),), jnp.float32)
    old_moment = scatter_about(key_of[3], (N_DP * BUCKET,), 0.5, 6.0, ((0, 128),), jnp.float32)
    old_variance = jnp.clip(jnp.exp(math.log(8.0) - 2.7725887 * jax.random.uniform(key_of[4], (N_DP * BUCKET,), jnp.float32) ** shard_levels(key_of[4], (N_DP * BUCKET,), ((0, 128),), -0.2, 0.2)), 0.5, 8.0)
    old_bounds = draw_old_bounds(jax.random.fold_in(key_of[6], 71), 0)
    return dict(grad_query=grad_query, grad_gate=grad_gate, old_master=old_master, old_moment=old_moment, old_variance=old_variance, old_bounds=old_bounds)


beta_one = 0.9
beta_two = 0.95
learn_rate = 0.01
decay_rate = 0.1
epsilon = 1e-08

def adamw_step(master, moment, variance, grad):
    moment_new = beta_one * moment + (1.0 - beta_one) * grad
    variance_new = beta_two * variance + (1.0 - beta_two) * grad * grad
    corrected_m = moment_new / (1.0 - beta_one ** STEP)
    corrected_v = variance_new / (1.0 - beta_two ** STEP)
    master_new = master - learn_rate * (corrected_m / (jnp.sqrt(corrected_v) + epsilon) + decay_rate * master)
    return (master_new, moment_new, variance_new)

def reference(grad_query, grad_gate, old_master, old_moment, old_variance, old_bounds):

    def accumulate(carry, pieces):
        part_q, part_g = pieces
        return ((carry[0] + part_q.astype(jnp.float32), carry[1] + part_g.astype(jnp.float32)), None)
    zeros = (jnp.zeros(grad_query.shape[1:], jnp.float32), jnp.zeros(grad_gate.shape[1:], jnp.float32))
    (sum_query, sum_gate), _ = lax.scan(accumulate, zeros, (grad_query, grad_gate))
    flat_grad = jnp.concatenate([sum_query.reshape(-1), sum_gate.reshape(-1)])
    positions = jnp.arange(PARAMS).astype(jnp.int32)
    bound_rows = old_bounds.reshape(N_DP // 4, 4, 2)[:, :3, :].reshape(OLD, 2)
    starts = bound_rows[:, 0].astype(jnp.int32)
    old_owner = (jnp.searchsorted(starts, positions, side='right') - 1).astype(jnp.int32)
    holder = (4 * (old_owner // 3) + old_owner % 3).astype(jnp.int32)
    slots = holder * BUCKET + positions - starts[old_owner]
    master = old_master[slots]
    moment = old_moment[slots]
    variance = old_variance[slots]
    master_new, moment_new, variance_new = adamw_step(master, moment, variance, flat_grad)
    weights = master_new.astype(jnp.bfloat16)
    query_weight = weights[:QROWS * D].reshape(QROWS, D)
    gate_weight = weights[QROWS * D:].reshape(GROWS, D)
    return (master_new, moment_new, variance_new, query_weight, gate_weight)
```

```python
import functools

import jax
import jax.numpy as jnp
from jax import lax
from jax.experimental import pallas as pl
from jax.experimental.pallas import tpu as pltpu
from jax.sharding import PartitionSpec as P

MESH = pl.DeviceIdType.MESH
F32 = jnp.float32
BF16 = jnp.bfloat16

STEP = 10
beta_one = 0.9
beta_two = 0.95
learn_rate = 0.01
decay_rate = 0.1
epsilon = 1e-08

LANE = 128
BLK = 32
ORDER = ((0, 1, 2), (1, 2, 0), (2, 0, 1))


def adamw_step(master, moment, variance, grad):
    moment_new = beta_one * moment + (1.0 - beta_one) * grad
    variance_new = beta_two * variance + (1.0 - beta_two) * grad * grad
    corrected_m = moment_new / (1.0 - beta_one**STEP)
    corrected_v = variance_new / (1.0 - beta_two**STEP)
    master_new = master - learn_rate * (
        corrected_m / (jnp.sqrt(corrected_v) + epsilon) + decay_rate * master
    )
    return (master_new, moment_new, variance_new)


def kernel(
    stop,
    query, gate, old_m, old_v, old_s, bounds,
    new_m, new_v, new_s, weights,
    mine, other, s0, r1, s1, r2, s2, r3, state, passed, arrived,
    load_sem, s0_send, s0_recv, s1_send, s1_recv, s2_send, s2_recv, s3_send, s3_recv,
    x_send, x_recv, g_send, g_recv, c_send, c_recv, p_send, p_recv,
):
    me = lax.axis_index("dp")
    core = me % 2
    chip = me // 2
    at = (chip // 16, (chip // 4) % 4, chip % 4)
    sibling = me + 1 - 2 * core

    def device(axis, by, on_core):
        place = list(at)
        place[axis] = (place[axis] + by) % 4
        return ((place[0] * 4 + place[1]) * 4 + place[2]) * 2 + on_core

    def remote(src, dst, send, recv, to):
        return pltpu.make_async_remote_copy(
            src_ref=src, dst_ref=dst, send_sem=send, recv_sem=recv,
            device_id=(to,), device_id_type=MESH,
        )

    sent = []

    loads = [
        pltpu.make_async_copy(query.at[:, core], mine.at[pl.ds(0, 64)], load_sem.at[0]),
        pltpu.make_async_copy(gate.at[:, core], mine.at[pl.ds(64, 128)], load_sem.at[1]),
    ]
    for n, old in enumerate((old_m, old_v, old_s)):
        loads.append(
            pltpu.make_async_copy(old, state.at[n, pl.ds(96, 176)], load_sem.at[2 + n])
        )
    for copy in loads:
        copy.start()

    barrier = pltpu.get_barrier_semaphore()

    def greet(to):
        pl.semaphore_signal(barrier, inc=1, device_id=(to,), device_id_type=MESH)

    greet(sibling)
    for axis in range(3):
        for by in (1, 2, 3):
            greet(device(axis, by, core))

    @pl.when(core == 0)
    def _():
        for by in (1, 2, 3):
            greet(device(2, by, 1))

    @pl.when(core == 1)
    def _():
        for by in (1, 2, 3):
            greet(device(1, by, 0))

    pl.semaphore_wait(barrier, 13)

    swaps = [
        remote(query.at[:, 1 - core], other.at[pl.ds(0, 64)], s0_send.at[0], s0_recv.at[0], sibling),
        remote(gate.at[:, 1 - core], other.at[pl.ds(64, 128)], s0_send.at[1], s0_recv.at[1], sibling),
    ]
    for copy in swaps:
        copy.start()
    sent += swaps

    for n in range(3):
        state[n, pl.ds(0, 96)] = jnp.zeros((96, LANE), F32)
        state[n, pl.ds(272, 96)] = jnp.zeros((96, LANE), F32)
    for copy in loads[2:]:
        copy.wait()
    first = bounds[0, 0] // LANE
    last = bounds[0, 1] // LANE

    def window(n, base):
        rows = lax.broadcasted_iota(jnp.int32, (96, LANE), 0) + base
        piece = state[n, pl.ds(jnp.clip(base - first + 96, 0, 272), 96)]
        return jnp.where((rows >= first) & (rows < last), piece, 0.0)

    for n in range(3):
        passed[n] = window(n, (me + 1) * 96)
    hands_on = (core == 0) | (at[2] % 2 == 0)
    takes = (core == 1) | (at[2] % 2 == 1)
    handed = remote(
        passed, arrived, p_send.at[0], p_recv.at[0],
        sibling * (1 - core) + device(2, 1, 0) * core,
    )

    @pl.when(hands_on)
    def _():
        handed.start()

    for copy in loads[:2]:
        copy.wait()
    for copy in swaps:
        copy.wait_recv()

    def pair(i, carry):
        i_x, i_y = i // 4, i % 4
        for z in range(4):
            to = (4 * i + z, i_y * 16 + z * 4 + i_x, z * 16 + i_x * 4 + i_y)
            for p in range(3):
                row = 12 * i + 3 * z + p
                s0[p, to[p]] = mine[row].astype(F32) + other[row].astype(F32)
        return carry

    lax.fori_loop(0, 16, pair, 0)
    if stop == 0:
        return finish(stop, sent, handed, hands_on, takes, new_m, new_v, new_s, weights, s0)

    copies1 = {}
    for by in (2, 1, 3):
        for p in range(3):
            a = ORDER[p][0]
            copies1[p, by] = remote(
                s0.at[p, pl.ds((at[a] + by) % 4 * 16, 16)], r1.at[p, by - 1],
                s1_send.at[p * 3 + by - 1], s1_recv.at[p * 3 + by - 1], device(a, by, core),
            )
            copies1[p, by].start()
            sent.append(copies1[p, by])
    copies2 = {}
    for p in range(3):
        a, b, _ = ORDER[p]
        for by in (1, 2, 3):
            copies1[p, by].wait_recv()
        own = at[a] * 16

        def second(i, carry, p=p, own=own):
            s1[p, i] = (s0[p, own + i] + r1[p, 0, i]) + (r1[p, 1, i] + r1[p, 2, i])
            return carry

        lax.fori_loop(0, 16, second, 0)
        if stop == 1:
            continue
        for by in (2, 1, 3):
            copies2[p, by] = remote(
                s1.at[p, pl.ds((at[b] + by) % 4 * 4, 4)], r2.at[p, by - 1],
                s2_send.at[p * 3 + by - 1], s2_recv.at[p * 3 + by - 1], device(b, by, core),
            )
            copies2[p, by].start()
            sent.append(copies2[p, by])
    if stop == 1:
        return finish(stop, sent, handed, hands_on, takes, new_m, new_v, new_s, weights, s0)

    for p in range(3):
        _, b, c = ORDER[p]
        for by in (1, 2, 3):
            copies2[p, by].wait_recv()
        for i in range(4):
            own = at[b] * 4 + i
            s2[p, i] = (s1[p, own] + r2[p, 0, i]) + (r2[p, 1, i] + r2[p, 2, i])
        if stop == 2:
            continue
        unit = 2 * p + core
        owner = unit // 3
        place = unit % 3
        for by in (2, 1, 3):
            copy = remote(
                s2.at[p, (at[c] + by) % 4], r3.at[place, at[c]],
                s3_send.at[p * 4 + by], s3_recv.at[place * 4 + at[c]], device(c, by, owner),
            )
            copy.start()
            sent.append(copy)

        if p != 1:
            local = remote(
                s2.at[p, at[c]], r3.at[place, at[c]],
                s3_send.at[p * 4], s3_recv.at[place * 4 + at[c]], sibling,
            )
            crosses = core == (1 if p == 0 else 0)

            @pl.when(crosses)
            def _(local=local):
                local.start()
                local.wait_send()

            @pl.when(jnp.logical_not(crosses))
            def _(p=p, place=place, c=c):
                r3[place, at[c]] = s2[p, at[c]]
        else:
            r3[place, at[c]] = s2[p, at[c]]
    if stop == 2:
        return finish(stop, sent, handed, hands_on, takes, new_m, new_v, new_s, weights, s0)

    @pl.when(takes)
    def _():
        handed.wait_recv()

    @pl.when(jnp.logical_not(takes))
    def _():
        arrived[...] = jnp.zeros_like(arrived)

    own_state = [window(n, me * 96) + arrived[n] for n in range(3)]
    for n, ref in enumerate((new_m, new_v, new_s)):
        ref[...] = own_state[n]

    last_at = (
        at[2] * (1 - core) + at[0] * core,
        at[2] * (1 - core) + at[1] * core,
        at[0] * (1 - core) + at[1] * core,
    )
    gathers = {}
    for m in range(3):
        for by in range(4):
            if by == 0 and m != 1:
                continue
            src = (last_at[m] + by) % 4
            remote(
                r3.at[m, src], r3.at[m, src], s3_send.at[0], s3_recv.at[m * 4 + src], sibling
            ).wait_recv()
        rows = pl.ds(m * BLK, BLK)
        grad = (r3[m, 0] + r3[m, 1]) + (r3[m, 2] + r3[m, 3])
        master, moment, variance = adamw_step(new_m[rows], new_v[rows], new_s[rows], grad)
        new_m[rows] = master
        new_v[rows] = moment
        new_s[rows] = variance
        weights[at[0], at[1], at[2], 3 * core + m] = master.astype(BF16)
        if stop == 3:
            continue
        c = ORDER[m][2]
        block = weights.at[at[0], at[1], at[2], 3 * core + m]
        for by in (2, 1, 3):
            gathers[m, by] = remote(
                block, block, g_send.at[m * 3 + by - 1], g_recv.at[m * 3 + by - 1], device(c, by, core)
            )
            gathers[m, by].start()
            sent.append(gathers[m, by])
    if stop == 3:
        return finish(stop, sent, handed, hands_on, takes, new_m, new_v, new_s, weights, s0)

    def slab(m, free, where):
        index = [slice(None) if axis in free else where[axis] for axis in range(3)]
        return weights.at[index[0], index[1], index[2], 3 * core + m]

    def moved(axis, by):
        place = list(at)
        place[axis] = (place[axis] - by) % 4
        return place

    def await_slab(m, free, axis, by, sem):
        src = slab(m, free, moved(axis, by))
        remote(src, src, g_send.at[0], sem, sibling).wait_recv()

    for level in (1, 2):
        for m in range(3):
            a, b, c = ORDER[m]
            before, axis = ((c, b) if level == 1 else (b, a))
            held = () if level == 1 else (c,)
            for by in (1, 2, 3):
                await_slab(m, held, before, by, g_recv.at[(level - 1) * 9 + m * 3 + by - 1])
            free = held + (before,)
            block = slab(m, free, at)
            for by in (2, 1, 3):
                number = level * 9 + m * 3 + by - 1
                copy = remote(
                    block, block, g_send.at[number], g_recv.at[number], device(axis, by, core)
                )
                copy.start()
                sent.append(copy)
            if level == 2:
                copy = remote(block, block, c_send.at[m * 4], c_recv.at[m * 4], sibling)
                copy.start()
                sent.append(copy)
    if stop == 4:
        for m in range(3):
            a, b, c = ORDER[m]
            for by in (1, 2, 3):
                await_slab(m, (b, c), a, by, g_recv.at[18 + m * 3 + by - 1])
            src = slab(m, (b, c), at)
            remote(src, src, c_send.at[0], c_recv.at[m * 4], sibling).wait_recv()
        return finish(stop, sent, handed, hands_on, takes, new_m, new_v, new_s, weights, s0)
    for by in (1, 3, 2):
        for m in range(3):
            a, b, c = ORDER[m]
            await_slab(m, (b, c), a, by, g_recv.at[18 + m * 3 + by - 1])
            block = slab(m, (b, c), moved(a, by))
            copy = remote(block, block, c_send.at[m * 4 + by], c_recv.at[m * 4 + by], sibling)
            copy.start()
            sent.append(copy)
    for m in range(3):
        a, b, c = ORDER[m]
        for by in range(4):
            index = moved(a, by)
            index = [slice(None) if axis in (b, c) else index[axis] for axis in range(3)]
            src = weights.at[index[0], index[1], index[2], 3 * (1 - core) + m]
            remote(src, src, c_send.at[0], c_recv.at[m * 4 + by], sibling).wait_recv()
    finish(stop, sent, handed, hands_on, takes, None, None, None, None, None)


def finish(stop, sent, handed, hands_on, takes, new_m, new_v, new_s, weights, s0):
    for copy in sent:
        copy.wait_send()

    @pl.when(hands_on)
    def _():
        handed.wait_send()

    if stop < 3:
        @pl.when(takes)
        def _():
            handed.wait_recv()
        for ref in (new_m, new_v, new_s):
            ref[...] = jnp.zeros_like(ref)
        weights[0, 0, 0, 0] = s0[0, 0].astype(BF16)


def on_device(grad_query, grad_gate, old_master, old_moment, old_variance, old_bounds, stop=9):
    query_rows, row_width = grad_query.shape[1:]
    gate_rows = grad_gate.shape[1]
    query = grad_query.reshape(query_rows, 2, BLK, LANE)
    gate = grad_gate.reshape(gate_rows, 2, BLK, LANE)
    old = [a.reshape(-1, LANE) for a in (old_master, old_moment, old_variance)]
    any_space = pl.BlockSpec(memory_space=pl.ANY)
    vmem = pl.BlockSpec(memory_space=pltpu.VMEM)
    dma = pltpu.SemaphoreType.DMA
    shard = jax.ShapeDtypeStruct((96, LANE), F32)
    new_m, new_v, new_s, weights = pl.pallas_call(
        functools.partial(kernel, stop),
        out_shape=(shard, shard, shard, jax.ShapeDtypeStruct((4, 4, 4, 6, BLK, LANE), BF16)),
        in_specs=[any_space] * 5 + [pl.BlockSpec(memory_space=pltpu.SMEM)],
        out_specs=(vmem, vmem, vmem, vmem),
        scratch_shapes=[
            pltpu.VMEM((192, BLK, LANE), BF16),
            pltpu.VMEM((192, BLK, LANE), BF16),
            pltpu.VMEM((3, 64, BLK, LANE), F32),
            pltpu.VMEM((3, 3, 16, BLK, LANE), F32),
            pltpu.VMEM((3, 16, BLK, LANE), F32),
            pltpu.VMEM((3, 3, 4, BLK, LANE), F32),
            pltpu.VMEM((3, 4, BLK, LANE), F32),
            pltpu.VMEM((3, 4, BLK, LANE), F32),
            pltpu.VMEM((3, 368, LANE), F32),
            pltpu.VMEM((3, 96, LANE), F32),
            pltpu.VMEM((3, 96, LANE), F32),
            dma((5,)),
            dma((2,)), dma((2,)),
            dma((9,)), dma((9,)),
            dma((9,)), dma((9,)),
            dma((12,)), dma((12,)),
            dma((1,)), dma((1,)),
            dma((27,)), dma((27,)),
            dma((12,)), dma((12,)),
            dma((1,)), dma((1,)),
        ],
        compiler_params=pltpu.CompilerParams(
            collective_id=0, has_side_effects=True, vmem_limit_bytes=40 * 1024 * 1024
        ),
    )(query, gate, *old, old_bounds)
    flat = weights.reshape(-1)
    split = query_rows * row_width
    return (
        new_m.reshape(-1), new_v.reshape(-1), new_s.reshape(-1),
        flat[:split].reshape(query_rows, row_width),
        flat[split:].reshape(gate_rows, row_width),
    )


def solution(mesh, stop=9):
    placed = (P("dp", None, None), P("dp", None, None), P("dp"), P("dp"), P("dp"), P("dp", None))
    return jax.shard_map(
        functools.partial(on_device, stop=stop),
        mesh=mesh,
        in_specs=placed,
        out_specs=(P("dp"), P("dp"), P("dp"), P(), P()),
        check_vma=False,
    )
```

```python
import functools

import jax
import jax.numpy as jnp
from jax import lax
from jax.experimental import pallas as pl
from jax.experimental.pallas import tpu as pltpu
from jax.sharding import PartitionSpec as P

MESH = pl.DeviceIdType.MESH
F32 = jnp.float32
BF16 = jnp.bfloat16

STEP = 10
beta_one = 0.9
beta_two = 0.95
learn_rate = 0.01
decay_rate = 0.1
epsilon = 1e-08

LANE = 128
PITCH = 40
BLK = 32
ORDER = ((0, 1, 2), (1, 2, 0), (2, 0, 1))


def adamw_step(master, moment, variance, grad):
    moment_new = beta_one * moment + (1.0 - beta_one) * grad
    variance_new = beta_two * variance + (1.0 - beta_two) * grad * grad
    corrected_m = moment_new / (1.0 - beta_one**STEP)
    corrected_v = variance_new / (1.0 - beta_two**STEP)
    master_new = master - learn_rate * (
        corrected_m / (jnp.sqrt(corrected_v) + epsilon) + decay_rate * master
    )
    return (master_new, moment_new, variance_new)


def kernel(
    stop,
    query, gate, old_m, old_v, old_s, bounds,
    new_m, new_v, new_s, weights,
    mine, other, s0, r1, s1, r2, s2, r3, state, passed, arrived,
    load_sem, s0_send, s0_recv, s1_send, s1_recv, s2_send, s2_recv, s3_send, s3_recv,
    x_send, x_recv, g_send, g_recv, c_send, c_recv, p_send, p_recv,
):
    me = lax.axis_index("dp")
    core = me % 2
    chip = me // 2
    at = (chip // 16, (chip // 4) % 4, chip % 4)
    sibling = me + 1 - 2 * core

    def device(axis, by, on_core):
        place = list(at)
        place[axis] = (place[axis] + by) % 4
        return ((place[0] * 4 + place[1]) * 4 + place[2]) * 2 + on_core

    def remote(src, dst, send, recv, to):
        return pltpu.make_async_remote_copy(
            src_ref=src, dst_ref=dst, send_sem=send, recv_sem=recv,
            device_id=(to,), device_id_type=MESH,
        )

    sent = []

    half = mine.shape[1]
    pieces = ((query, 0, 0, 48), (query, 48, 48, 16), (gate, 0, 64, 32), (gate, 32, 96, 48), (gate, 80, 144, 48))
    of_chunk = ((0,), (1, 2), (3,), (4,))
    own_half = pl.ds(pl.multiple_of(core * half, half), half)
    its_half = pl.ds(pl.multiple_of((1 - core) * half, half), half)
    loads, olds, swaps = [], [], []
    for n, (array, start, row, rows) in enumerate(pieces):
        loads.append(pltpu.make_async_copy(
            array.at[pl.ds(start, rows), own_half], mine.at[pl.ds(row, rows)], load_sem.at[n]))
        swaps.append(remote(
            array.at[pl.ds(start, rows), its_half], other.at[pl.ds(row, rows)],
            s0_send.at[n], s0_recv.at[n], sibling))
    for n, old in enumerate((old_m, old_v, old_s)):
        olds.append(
            pltpu.make_async_copy(old, state.at[n, pl.ds(96, 176)], load_sem.at[5 + n])
        )
    for copy in loads + olds:
        copy.start()

    barrier = pltpu.get_barrier_semaphore()

    def greet(to):
        pl.semaphore_signal(barrier, inc=1, device_id=(to,), device_id_type=MESH)

    greet(sibling)
    for axis in range(3):
        for by in (1, 2, 3):
            greet(device(axis, by, core))

    @pl.when(core == 0)
    def _():
        for by in (1, 2, 3):
            greet(device(2, by, 1))

    @pl.when(core == 1)
    def _():
        for by in (1, 2, 3):
            greet(device(1, by, 0))

    pl.semaphore_wait(barrier, 13)

    for copy in swaps:
        copy.start()
    sent += swaps

    hands_on = (core == 0) | (at[2] % 2 == 0)
    takes = (core == 1) | (at[2] % 2 == 1)
    handed = remote(
        passed, arrived, p_send.at[0], p_recv.at[0],
        sibling * (1 - core) + device(2, 1, 0) * core,
    )

    flat0 = s0.reshape(192 * PITCH, LANE)
    blocks0 = s0.reshape(4, 4, 4, 3, PITCH, LANE)
    rows0 = pl.ds(0, BLK)
    by_first = {}
    for x in range(4):
        for n in of_chunk[x]:
            loads[n].wait()
            swaps[n].wait_recv()

        def pair(i, carry):
            row = pl.multiple_of(48 * x + 16 * i, 16)
            for j in range(BLK):
                lanes = pl.ds(j * LANE, LANE)
                both = mine[pl.ds(row, 16), lanes].astype(F32) + other[pl.ds(row, 16), lanes].astype(F32)
                flat0[pl.ds(row * PITCH + j, 16, stride=PITCH), :] = both
            return carry

        lax.fori_loop(0, 3, pair, 0)
        if stop == 0:
            continue

        @pl.when(at[0] != x)
        def _(x=x):
            by = (x - at[0] + 4) % 4
            remote(
                blocks0.at[x, :, :, 0, rows0], r1.at[0, by - 1],
                s1_send.at[by - 1], s1_recv.at[by - 1], device(0, by, core),
            ).start()

        for by in (2, 1, 3):
            n = 3 + x * 6 + by - 1
            to_y, to_z = (at[1] + by) % 4, (at[2] + by) % 4
            by_first[1, x, by] = remote(
                blocks0.at[x, to_y, :, 1, rows0], r1.at[1, by - 1, x],
                s1_send.at[n], s1_recv.at[n], device(1, by, core),
            )
            by_first[2, x, by] = remote(
                blocks0.at[x, :, to_z, 2, rows0], r1.at[2, by - 1, x],
                s1_send.at[n + 3], s1_recv.at[n + 3], device(2, by, core),
            )
            for p in (1, 2):
                by_first[p, x, by].start()
                sent.append(by_first[p, x, by])
    for by in (1, 2, 3):
        by_first[0, 0, by] = remote(
            blocks0.at[0, :, :, 0, rows0], r1.at[0, by - 1],
            s1_send.at[by - 1], s1_recv.at[by - 1], device(0, by, core),
        )
        if stop > 0:
            sent.append(by_first[0, 0, by])

    for n in range(3):
        state[n, pl.ds(0, 96)] = jnp.zeros((96, LANE), F32)
        state[n, pl.ds(272, 96)] = jnp.zeros((96, LANE), F32)
    for copy in olds:
        copy.wait()
    first = bounds[0, 0] // LANE
    last = bounds[0, 1] // LANE

    def window(n, base):
        rows = lax.broadcasted_iota(jnp.int32, (96, LANE), 0) + base
        piece = state[n, pl.ds(jnp.clip(base - first + 96, 0, 272), 96)]
        return jnp.where((rows >= first) & (rows < last), piece, 0.0)

    for n in range(3):
        passed[n] = window(n, (me + 1) * 96)

    @pl.when(hands_on)
    def _():
        handed.start()

    for n, ref in enumerate((new_m, new_v, new_s)):
        ref[...] = window(n, me * 96)

    if stop == 0:
        return finish(stop, sent, handed, hands_on, takes, new_m, new_v, new_s, weights, s0)

    copies2 = {}
    for p in range(3):
        a, b, _ = ORDER[p]
        for by in (1, 2, 3):
            for x in (range(4) if p else (0,)):
                by_first[p, x, by].wait_recv()

        def second(i, carry, p=p):
            for k in range(4):
                if p == 0:
                    own, to = (at[0], i, k, 0), i * 4 + k
                elif p == 1:
                    own, to = (i, at[1], k, 1), k * 4 + i
                else:
                    own, to = (i, k, at[2], 2), i * 4 + k
                own = blocks0[own + (rows0,)]
                s1[p, to] = (own + r1[p, 0, i, k]) + (r1[p, 1, i, k] + r1[p, 2, i, k])
            return carry

        lax.fori_loop(0, 4, second, 0)
        if stop == 1:
            continue
        for by in (2, 1, 3):
            copies2[p, by] = remote(
                s1.at[p, pl.ds((at[b] + by) % 4 * 4, 4)], r2.at[p, by - 1],
                s2_send.at[p * 3 + by - 1], s2_recv.at[p * 3 + by - 1], device(b, by, core),
            )
            copies2[p, by].start()
            sent.append(copies2[p, by])
    if stop == 1:
        return finish(stop, sent, handed, hands_on, takes, new_m, new_v, new_s, weights, s0)

    for p in range(3):
        _, b, c = ORDER[p]
        for by in (1, 2, 3):
            copies2[p, by].wait_recv()
        for i in range(4):
            own = at[b] * 4 + i
            s2[p, i] = (s1[p, own] + r2[p, 0, i]) + (r2[p, 1, i] + r2[p, 2, i])
        if stop == 2:
            continue
        unit = 2 * p + core
        owner = unit // 3
        place = unit % 3
        for by in (2, 1, 3):
            copy = remote(
                s2.at[p, (at[c] + by) % 4], r3.at[place, at[c]],
                s3_send.at[p * 4 + by], s3_recv.at[place * 4 + at[c]], device(c, by, owner),
            )
            copy.start()
            sent.append(copy)

        if p != 1:
            local = remote(
                s2.at[p, at[c]], r3.at[place, at[c]],
                s3_send.at[p * 4], s3_recv.at[place * 4 + at[c]], sibling,
            )
            crosses = core == (1 if p == 0 else 0)

            @pl.when(crosses)
            def _(local=local):
                local.start()
                local.wait_send()

            @pl.when(jnp.logical_not(crosses))
            def _(p=p, place=place, c=c):
                r3[place, at[c]] = s2[p, at[c]]
        else:
            r3[place, at[c]] = s2[p, at[c]]
    if stop == 2:
        return finish(stop, sent, handed, hands_on, takes, new_m, new_v, new_s, weights, s0)

    @pl.when(takes)
    def _():
        handed.wait_recv()

    @pl.when(jnp.logical_not(takes))
    def _():
        arrived[...] = jnp.zeros_like(arrived)

    for n, ref in enumerate((new_m, new_v, new_s)):
        ref[...] += arrived[n]

    last_at = (
        at[2] * (1 - core) + at[0] * core,
        at[2] * (1 - core) + at[1] * core,
        at[0] * (1 - core) + at[1] * core,
    )
    gathers = {}
    for m in range(3):
        for by in range(4):
            if by == 0 and m != 1:
                continue
            src = (last_at[m] + by) % 4
            remote(
                r3.at[m, src], r3.at[m, src], s3_send.at[0], s3_recv.at[m * 4 + src], sibling
            ).wait_recv()
        rows = pl.ds(m * BLK, BLK)
        grad = (r3[m, 0] + r3[m, 1]) + (r3[m, 2] + r3[m, 3])
        master, moment, variance = adamw_step(new_m[rows], new_v[rows], new_s[rows], grad)
        new_m[rows] = master
        new_v[rows] = moment
        new_s[rows] = variance
        weights[at[0], at[1], at[2], 3 * core + m] = master.astype(BF16)
        if stop == 3:
            continue
        c = ORDER[m][2]
        block = weights.at[at[0], at[1], at[2], 3 * core + m]
        for by in (2, 1, 3):
            gathers[m, by] = remote(
                block, block, g_send.at[m * 3 + by - 1], g_recv.at[m * 3 + by - 1], device(c, by, core)
            )
            gathers[m, by].start()
            sent.append(gathers[m, by])
    if stop == 3:
        return finish(stop, sent, handed, hands_on, takes, new_m, new_v, new_s, weights, s0)

    def slab(m, free, where):
        index = [slice(None) if axis in free else where[axis] for axis in range(3)]
        return weights.at[index[0], index[1], index[2], 3 * core + m]

    def moved(axis, by):
        place = list(at)
        place[axis] = (place[axis] - by) % 4
        return place

    def await_slab(m, free, axis, by, sem):
        src = slab(m, free, moved(axis, by))
        remote(src, src, g_send.at[0], sem, sibling).wait_recv()

    for level in (1, 2):
        for m in range(3):
            a, b, c = ORDER[m]
            before, axis = ((c, b) if level == 1 else (b, a))
            held = () if level == 1 else (c,)
            for by in (1, 2, 3):
                await_slab(m, held, before, by, g_recv.at[(level - 1) * 9 + m * 3 + by - 1])
            free = held + (before,)
            block = slab(m, free, at)
            for by in (2, 1, 3):
                number = level * 9 + m * 3 + by - 1
                copy = remote(
                    block, block, g_send.at[number], g_recv.at[number], device(axis, by, core)
                )
                copy.start()
                sent.append(copy)
            if level == 2:
                copy = remote(block, block, c_send.at[m * 4], c_recv.at[m * 4], sibling)
                copy.start()
                sent.append(copy)
    if stop == 4:
        for m in range(3):
            a, b, c = ORDER[m]
            for by in (1, 2, 3):
                await_slab(m, (b, c), a, by, g_recv.at[18 + m * 3 + by - 1])
            src = slab(m, (b, c), at)
            remote(src, src, c_send.at[0], c_recv.at[m * 4], sibling).wait_recv()
        return finish(stop, sent, handed, hands_on, takes, new_m, new_v, new_s, weights, s0)
    for by in (1, 3, 2):
        for m in range(3):
            a, b, c = ORDER[m]
            await_slab(m, (b, c), a, by, g_recv.at[18 + m * 3 + by - 1])
            block = slab(m, (b, c), moved(a, by))
            copy = remote(block, block, c_send.at[m * 4 + by], c_recv.at[m * 4 + by], sibling)
            copy.start()
            sent.append(copy)
    for m in range(3):
        a, b, c = ORDER[m]
        for by in range(4):
            index = moved(a, by)
            index = [slice(None) if axis in (b, c) else index[axis] for axis in range(3)]
            src = weights.at[index[0], index[1], index[2], 3 * (1 - core) + m]
            remote(src, src, c_send.at[0], c_recv.at[m * 4 + by], sibling).wait_recv()
    finish(stop, sent, handed, hands_on, takes, None, None, None, None, None)


def finish(stop, sent, handed, hands_on, takes, new_m, new_v, new_s, weights, s0):
    for copy in sent:
        copy.wait_send()

    @pl.when(hands_on)
    def _():
        handed.wait_send()

    if stop < 3:
        @pl.when(takes)
        def _():
            handed.wait_recv()
        for ref in (new_m, new_v, new_s):
            ref[...] = jnp.zeros_like(ref)
        weights[0, 0, 0, 0] = s0[0, pl.ds(0, BLK)].astype(BF16)


def write(weights, new_m, new_v, new_s, query, gate, out_m, out_v, out_s, tiles, sems):
    split, rows = query.shape[0], tiles.shape[0]
    copies = [
        pltpu.make_async_copy(src, dst, sems.at[rows // 16 + n])
        for n, (src, dst) in enumerate(((new_m, out_m), (new_v, out_v), (new_s, out_s)))
    ]

    def group(i, carry):
        at = pl.ds(pl.multiple_of(16 * i, 16), 16)
        for j in range(0, weights.shape[1], 8):
            block = jnp.swapaxes(weights[at, pl.ds(j, 8)], 0, 1)
            for k in range(8):
                tiles[at, pl.ds((j + k) * LANE, LANE)] = block[k]

        @pl.when(i < split // 16)
        def _():
            pltpu.make_async_copy(tiles.at[at], query.at[at], sems.at[i]).start()

        @pl.when(i >= split // 16)
        def _():
            to = pl.ds(pl.multiple_of(16 * i - split, 16), 16)
            pltpu.make_async_copy(tiles.at[at], gate.at[to], sems.at[i]).start()

        return carry

    for copy in copies:
        copy.start()
    lax.fori_loop(0, rows // 16, group, 0)
    for i in range(rows // 16):
        to = query.at[pl.ds(16 * i, 16)] if 16 * i < split else gate.at[pl.ds(16 * i - split, 16)]
        copies.append(pltpu.make_async_copy(tiles.at[pl.ds(16 * i, 16)], to, sems.at[i]))
    for copy in copies:
        copy.wait()


def on_device(grad_query, grad_gate, old_master, old_moment, old_variance, old_bounds, stop=9):
    query_rows, row_width = grad_query.shape[1:]
    gate_rows = grad_gate.shape[1]
    query = grad_query.reshape(query_rows, row_width)
    gate = grad_gate.reshape(gate_rows, row_width)
    old = [a.reshape(-1, LANE) for a in (old_master, old_moment, old_variance)]
    query, gate, *old = [
        pltpu.with_memory_space_constraint(a, pltpu.HBM) for a in (query, gate, *old)
    ]
    hbm = pl.BlockSpec(memory_space=pltpu.HBM)
    vmem = pl.BlockSpec(memory_space=pltpu.VMEM)
    dma = pltpu.SemaphoreType.DMA
    shard = jax.ShapeDtypeStruct((96, LANE), F32)
    rows = query_rows + gate_rows
    new_m, new_v, new_s, weights = pl.pallas_call(
        functools.partial(kernel, stop),
        out_shape=(
            pltpu.VMEM(shard.shape, F32), pltpu.VMEM(shard.shape, F32), pltpu.VMEM(shard.shape, F32),
            pltpu.VMEM((4, 4, 4, 6, BLK, LANE), BF16),
        ),
        in_specs=[hbm] * 5 + [pl.BlockSpec(memory_space=pltpu.SMEM)],
        out_specs=(vmem, vmem, vmem, vmem),
        scratch_shapes=[
            pltpu.VMEM((rows, row_width // 2), BF16),
            pltpu.VMEM((rows, row_width // 2), BF16),
            pltpu.VMEM((rows, PITCH, LANE), F32),
            pltpu.VMEM((3, 3, 4, 4, BLK, LANE), F32),
            pltpu.VMEM((3, 16, BLK, LANE), F32),
            pltpu.VMEM((3, 3, 4, BLK, LANE), F32),
            pltpu.VMEM((3, 4, BLK, LANE), F32),
            pltpu.VMEM((3, 4, BLK, LANE), F32),
            pltpu.VMEM((3, 368, LANE), F32),
            pltpu.VMEM((3, 96, LANE), F32),
            pltpu.VMEM((3, 96, LANE), F32),
            dma((8,)),
            dma((5,)), dma((5,)),
            dma((27,)), dma((27,)),
            dma((9,)), dma((9,)),
            dma((12,)), dma((12,)),
            dma((1,)), dma((1,)),
            dma((27,)), dma((27,)),
            dma((12,)), dma((12,)),
            dma((1,)), dma((1,)),
        ],
        compiler_params=pltpu.CompilerParams(
            collective_id=0, has_side_effects=True, vmem_limit_bytes=48 * 1024 * 1024
        ),
    )(query, gate, *old, old_bounds)
    query_new, gate_new, new_m, new_v, new_s = pl.pallas_call(
        write,
        out_shape=(
            jax.ShapeDtypeStruct((query_rows, row_width), BF16),
            jax.ShapeDtypeStruct((gate_rows, row_width), BF16),
            shard, shard, shard,
        ),
        in_specs=[vmem] * 4,
        out_specs=(hbm,) * 5,
        scratch_shapes=[pltpu.VMEM((rows, row_width), BF16), dma((rows // 16 + 3,))],
        compiler_params=pltpu.CompilerParams(vmem_limit_bytes=48 * 1024 * 1024),
    )(weights.reshape(rows, row_width // LANE, LANE), new_m, new_v, new_s)
    return (new_m.reshape(-1), new_v.reshape(-1), new_s.reshape(-1), query_new, gate_new)


def solution(mesh, stop=9):
    placed = (P("dp", None, None), P("dp", None, None), P("dp"), P("dp"), P("dp"), P("dp", None))
    return jax.shard_map(
        functools.partial(on_device, stop=stop),
        mesh=mesh,
        in_specs=placed,
        out_specs=(P("dp"), P("dp"), P("dp"), P(), P()),
        check_vma=False,
    )
```

```python
import functools

import jax
import jax.numpy as jnp
from jax import lax
from jax.experimental import pallas as pl
from jax.experimental.pallas import tpu as pltpu
from jax.sharding import PartitionSpec as P

MESH = pl.DeviceIdType.MESH
F32 = jnp.float32
BF16 = jnp.bfloat16

STEP = 10
beta_one = 0.9
beta_two = 0.95
learn_rate = 0.01
decay_rate = 0.1
epsilon = 1e-08

LANE = 128
PITCH = 40
BLK = 32
BOUND = (48.0, 192.0)
ORDER = ((0, 1, 2), (1, 2, 0), (2, 0, 1))


def adamw_step(master, moment, variance, grad):
    moment_new = beta_one * moment + (1.0 - beta_one) * grad
    variance_new = beta_two * variance + (1.0 - beta_two) * grad * grad
    corrected_m = moment_new / (1.0 - beta_one**STEP)
    corrected_v = variance_new / (1.0 - beta_two**STEP)
    master_new = master - learn_rate * (
        corrected_m / (jnp.sqrt(corrected_v) + epsilon) + decay_rate * master
    )
    return (master_new, moment_new, variance_new)


def encode(value, bound):
    ratio = jnp.maximum(jnp.abs(value), 1e-30) * (1.0 / bound)
    root = lax.rsqrt(lax.rsqrt(ratio))
    code = root * lax.rsqrt(root) * 32767.0
    return jnp.round(jnp.where(value < 0, -code, code)).astype(jnp.int32).astype(jnp.int16)


def decode(code, bound):
    root = code.astype(jnp.int32).astype(F32) * (bound**0.125 / 32767.0)
    square = root * root
    return (root * jnp.abs(root)) * (square * (square * square))


def kernel(
    stop,
    query, gate, old_m, old_v, old_s, bounds_hbm,
    new_m, new_v, new_s, weights,
    mine, other, s0, e0, r1, s1, e1, r2, s2, r3, state, passed, arrived, bounds,
    load_sem, s0_send, s0_recv, s1_send, s1_recv, s2_send, s2_recv, s3_send, s3_recv,
    x_send, x_recv, g_send, g_recv, c_send, c_recv, p_send, p_recv,
):
    me = lax.axis_index("dp")
    core = me % 2
    chip = me // 2
    at = (chip // 16, (chip // 4) % 4, chip % 4)
    sibling = me + 1 - 2 * core

    def device(axis, by, on_core):
        place = list(at)
        place[axis] = (place[axis] + by) % 4
        return ((place[0] * 4 + place[1]) * 4 + place[2]) * 2 + on_core

    def remote(src, dst, send, recv, to):
        return pltpu.make_async_remote_copy(
            src_ref=src, dst_ref=dst, send_sem=send, recv_sem=recv,
            device_id=(to,), device_id_type=MESH,
        )

    sent = []

    half = mine.shape[1]
    pieces = ((query, 0, 0, 48), (query, 48, 48, 16), (gate, 0, 64, 32), (gate, 32, 96, 48), (gate, 80, 144, 48))
    of_chunk = ((0,), (1, 2), (3,), (4,))
    own_half = pl.ds(pl.multiple_of(core * half, half), half)
    its_half = pl.ds(pl.multiple_of((1 - core) * half, half), half)
    loads, olds, swaps = [], [], []
    for n, (array, start, row, rows) in enumerate(pieces):
        loads.append(pltpu.make_async_copy(
            array.at[pl.ds(start, rows), own_half], mine.at[pl.ds(row, rows)], load_sem.at[n]))
        swaps.append(remote(
            array.at[pl.ds(start, rows), its_half], other.at[pl.ds(row, rows)],
            s0_send.at[n], s0_recv.at[n], sibling))
    for n, old in enumerate((old_m, old_v, old_s)):
        olds.append(
            pltpu.make_async_copy(old, state.at[n, pl.ds(96, 176)], load_sem.at[5 + n])
        )
    olds.append(pltpu.make_async_copy(bounds_hbm, bounds, load_sem.at[8]))
    for copy in olds + loads:
        copy.start()

    barrier = pltpu.get_barrier_semaphore()

    def greet(to):
        pl.semaphore_signal(barrier, inc=1, device_id=(to,), device_id_type=MESH)

    greet(sibling)
    for axis in range(3):
        for by in (1, 2, 3):
            greet(device(axis, by, core))

    @pl.when(core == 0)
    def _():
        for by in (1, 2, 3):
            greet(device(2, by, 1))

    @pl.when(core == 1)
    def _():
        for by in (1, 2, 3):
            greet(device(1, by, 0))

    for n in range(3):
        state[n, pl.ds(0, 96)] = jnp.zeros((96, LANE), F32)
        state[n, pl.ds(272, 96)] = jnp.zeros((96, LANE), F32)
    for copy in olds:
        copy.wait()
    first = bounds[0, 0] // LANE
    last = bounds[0, 1] // LANE

    def window(n, base):
        rows = lax.broadcasted_iota(jnp.int32, (96, LANE), 0) + base
        piece = state[n, pl.ds(jnp.clip(base - first + 96, 0, 272), 96)]
        return jnp.where((rows >= first) & (rows < last), piece, 0.0)

    for n in range(3):
        passed[n] = window(n, (me + 1) * 96)
    for n, ref in enumerate((new_m, new_v, new_s)):
        ref[...] = window(n, me * 96)

    pl.semaphore_wait(barrier, 13)

    for copy in swaps:
        copy.start()
    sent += swaps

    hands_on = (core == 0) | (at[2] % 2 == 0)
    takes = (core == 1) | (at[2] % 2 == 1)
    handed = remote(
        passed, arrived, p_send.at[0], p_recv.at[0],
        sibling * (1 - core) + device(2, 1, 0) * core,
    )

    @pl.when(hands_on)
    def _():
        handed.start()

    flat0 = s0.reshape(192 * PITCH, LANE)
    blocks0 = s0.reshape(4, 4, 4, 3, PITCH, LANE)
    rows0 = pl.ds(0, BLK)
    by_first = {}
    for x in range(4):
        for n in of_chunk[x]:
            loads[n].wait()
            swaps[n].wait_recv()

        def pair(i, carry):
            row = pl.multiple_of(48 * x + 16 * i, 16)
            for j in range(BLK):
                lanes = pl.ds(j * LANE, LANE)
                both = mine[pl.ds(row, 16), lanes].astype(F32) + other[pl.ds(row, 16), lanes].astype(F32)
                flat0[pl.ds(row * PITCH + j, 16, stride=PITCH), :] = both
            return carry

        lax.fori_loop(0, 3, pair, 0)
        if stop == 0:
            continue

        @pl.when(at[0] != x)
        def _(x=x):
            def code(i, carry):
                for k in range(4):
                    e0[0, x, i, k] = encode(blocks0[x, i, k, 0, rows0], BOUND[0])
                return carry

            lax.fori_loop(0, 4, code, 0)
            by = (x - at[0] + 4) % 4
            remote(
                e0.at[0, x], r1.at[0, by - 1],
                s1_send.at[by - 1], s1_recv.at[by - 1], device(0, by, core),
            ).start()

        def code(i, carry, x=x):
            for by in (1, 2, 3):
                to_y, to_z = (at[1] + by) % 4, (at[2] + by) % 4
                e0[1, to_y, x, i] = encode(blocks0[x, to_y, i, 1, rows0], BOUND[0])
                e0[2, to_z, x, i] = encode(blocks0[x, i, to_z, 2, rows0], BOUND[0])
            return carry

        lax.fori_loop(0, 4, code, 0)
        for by in (2, 1, 3):
            n = 3 + x * 6 + by - 1
            for p in (1, 2):
                by_first[p, x, by] = remote(
                    e0.at[p, (at[p] + by) % 4, x], r1.at[p, by - 1, x],
                    s1_send.at[n + 3 * p - 3], s1_recv.at[n + 3 * p - 3], device(p, by, core),
                )
                by_first[p, x, by].start()
                sent.append(by_first[p, x, by])
    for by in (1, 2, 3):
        by_first[0, 0, by] = remote(
            e0.at[0, 0], r1.at[0, by - 1],
            s1_send.at[by - 1], s1_recv.at[by - 1], device(0, by, core),
        )
        if stop > 0:
            sent.append(by_first[0, 0, by])

    if stop == 0:
        return finish(stop, sent, handed, hands_on, takes, new_m, new_v, new_s, weights, s0)

    copies2 = {}
    for p in range(3):
        a, b, _ = ORDER[p]
        for by in (1, 2, 3):
            for x in (range(4) if p else (0,)):
                by_first[p, x, by].wait_recv()

        def second(i, carry, p=p):
            for k in range(4):
                if p == 0:
                    own, to = (at[0], i, k, 0), i * 4 + k
                elif p == 1:
                    own, to = (i, at[1], k, 1), k * 4 + i
                else:
                    own, to = (i, k, at[2], 2), i * 4 + k
                total = blocks0[own + (rows0,)]
                for by in range(3):
                    total += decode(r1[p, by, i, k], BOUND[0])
                s1[p, to] = total
                e1[p, to] = encode(total, BOUND[1])
            return carry

        lax.fori_loop(0, 4, second, 0)
        if stop == 1:
            continue
        for by in (2, 1, 3):
            copies2[p, by] = remote(
                e1.at[p, pl.ds((at[b] + by) % 4 * 4, 4)], r2.at[p, by - 1],
                s2_send.at[p * 3 + by - 1], s2_recv.at[p * 3 + by - 1], device(b, by, core),
            )
            copies2[p, by].start()
            sent.append(copies2[p, by])
    if stop == 1:
        return finish(stop, sent, handed, hands_on, takes, new_m, new_v, new_s, weights, s0)

    for p in range(3):
        _, b, c = ORDER[p]
        for by in (1, 2, 3):
            copies2[p, by].wait_recv()
        for i in range(4):
            own = at[b] * 4 + i
            total = s1[p, own]
            for by in range(3):
                total += decode(r2[p, by, i], BOUND[1])
            s2[p, i] = total
        if stop == 2:
            continue
        unit = 2 * p + core
        owner = unit // 3
        place = unit % 3
        for by in (2, 1, 3):
            copy = remote(
                s2.at[p, (at[c] + by) % 4], r3.at[place, at[c]],
                s3_send.at[p * 4 + by], s3_recv.at[place * 4 + at[c]], device(c, by, owner),
            )
            copy.start()
            sent.append(copy)

        if p != 1:
            local = remote(
                s2.at[p, at[c]], r3.at[place, at[c]],
                s3_send.at[p * 4], s3_recv.at[place * 4 + at[c]], sibling,
            )
            crosses = core == (1 if p == 0 else 0)

            @pl.when(crosses)
            def _(local=local):
                local.start()
                local.wait_send()

            @pl.when(jnp.logical_not(crosses))
            def _(p=p, place=place, c=c):
                r3[place, at[c]] = s2[p, at[c]]
        else:
            r3[place, at[c]] = s2[p, at[c]]
    if stop == 2:
        return finish(stop, sent, handed, hands_on, takes, new_m, new_v, new_s, weights, s0)

    @pl.when(takes)
    def _():
        handed.wait_recv()

    @pl.when(jnp.logical_not(takes))
    def _():
        arrived[...] = jnp.zeros_like(arrived)

    for n, ref in enumerate((new_m, new_v, new_s)):
        ref[...] += arrived[n]

    last_at = (
        at[2] * (1 - core) + at[0] * core,
        at[2] * (1 - core) + at[1] * core,
        at[0] * (1 - core) + at[1] * core,
    )
    gathers = {}
    for m in range(3):
        for by in range(4):
            if by == 0 and m != 1:
                continue
            src = (last_at[m] + by) % 4
            remote(
                r3.at[m, src], r3.at[m, src], s3_send.at[0], s3_recv.at[m * 4 + src], sibling
            ).wait_recv()
        rows = pl.ds(m * BLK, BLK)
        grad = (r3[m, 0] + r3[m, 1]) + (r3[m, 2] + r3[m, 3])
        master, moment, variance = adamw_step(new_m[rows], new_v[rows], new_s[rows], grad)
        new_m[rows] = master
        new_v[rows] = moment
        new_s[rows] = variance
        weights[at[0], at[1], at[2], 3 * core + m] = master.astype(BF16)
        if stop == 3:
            continue
        c = ORDER[m][2]
        block = weights.at[at[0], at[1], at[2], 3 * core + m]
        for by in (2, 1, 3):
            gathers[m, by] = remote(
                block, block, g_send.at[m * 3 + by - 1], g_recv.at[m * 3 + by - 1], device(c, by, core)
            )
            gathers[m, by].start()
            sent.append(gathers[m, by])
    if stop == 3:
        return finish(stop, sent, handed, hands_on, takes, new_m, new_v, new_s, weights, s0)

    def slab(m, free, where):
        index = [slice(None) if axis in free else where[axis] for axis in range(3)]
        return weights.at[index[0], index[1], index[2], 3 * core + m]

    def moved(axis, by):
        place = list(at)
        place[axis] = (place[axis] - by) % 4
        return place

    def await_slab(m, free, where, sem):
        src = slab(m, free, where)
        remote(src, src, g_send.at[0], sem, sibling).wait_recv()

    def forward(m, by, block):
        copy = remote(block, block, c_send.at[m * 4 + by], c_recv.at[m * 4 + by], sibling)
        copy.start()
        sent.append(copy)

    def last_level(m, group):
        a, b, c = ORDER[m]
        block = slab(m, (c,), moved(b, group))
        for by in (2, 1, 3):
            number = 18 + m * 12 + group * 3 + by - 1
            copy = remote(
                block, block, g_send.at[number], g_recv.at[number], device(a, by, core)
            )
            copy.start()
            sent.append(copy)

    for m in range(3):
        a, b, c = ORDER[m]
        for by in (1, 2, 3):
            await_slab(m, (), moved(c, by), g_recv.at[m * 3 + by - 1])
        block = slab(m, (c,), at)
        for by in (2, 1, 3):
            number = 9 + m * 3 + by - 1
            copy = remote(
                block, block, g_send.at[number], g_recv.at[number], device(b, by, core)
            )
            copy.start()
            sent.append(copy)
        last_level(m, 0)
    for group in (1, 3, 2):
        for m in range(3):
            a, b, c = ORDER[m]
            await_slab(m, (c,), moved(b, group), g_recv.at[9 + m * 3 + group - 1])
            last_level(m, group)
    for m in range(3):
        forward(m, 0, slab(m, ORDER[m][1:], at))
    for by in (1, 3, 2):
        for m in range(3):
            a, b, c = ORDER[m]
            for group in (0, 1, 3, 2):
                place = moved(a, by)
                place[b] = (place[b] - group) % 4
                await_slab(m, (c,), place, g_recv.at[18 + m * 12 + group * 3 + by - 1])
            forward(m, by, slab(m, (b, c), moved(a, by)))
    for by in (0, 1, 3, 2):
        for m in range(3):
            a, b, c = ORDER[m]
            index = moved(a, by)
            index = [slice(None) if axis in (b, c) else index[axis] for axis in range(3)]
            src = weights.at[index[0], index[1], index[2], 3 * (1 - core) + m]
            remote(src, src, c_send.at[0], c_recv.at[m * 4 + by], sibling).wait_recv()
    finish(stop, sent, handed, hands_on, takes, None, None, None, None, None)


def finish(stop, sent, handed, hands_on, takes, new_m, new_v, new_s, weights, s0):
    for copy in sent:
        copy.wait_send()

    @pl.when(hands_on)
    def _():
        handed.wait_send()

    if stop < 3:
        @pl.when(takes)
        def _():
            handed.wait_recv()
        for ref in (new_m, new_v, new_s):
            ref[...] = jnp.zeros_like(ref)
        weights[0, 0, 0, 0] = s0[0, pl.ds(0, BLK)].astype(BF16)


def write(weights, new_m, new_v, new_s, query, gate, out_m, out_v, out_s, tiles, sems):
    split, rows = query.shape[0], tiles.shape[0]
    copies = [
        pltpu.make_async_copy(src, dst, sems.at[rows // 16 + n])
        for n, (src, dst) in enumerate(((new_m, out_m), (new_v, out_v), (new_s, out_s)))
    ]

    def group(i, carry):
        at = pl.ds(pl.multiple_of(16 * i, 16), 16)
        for j in range(0, weights.shape[1], 8):
            block = jnp.swapaxes(weights[at, pl.ds(j, 8)], 0, 1)
            for k in range(8):
                tiles[at, pl.ds((j + k) * LANE, LANE)] = block[k]

        @pl.when(i < split // 16)
        def _():
            pltpu.make_async_copy(tiles.at[at], query.at[at], sems.at[i]).start()

        @pl.when(i >= split // 16)
        def _():
            to = pl.ds(pl.multiple_of(16 * i - split, 16), 16)
            pltpu.make_async_copy(tiles.at[at], gate.at[to], sems.at[i]).start()

        return carry

    for copy in copies:
        copy.start()
    lax.fori_loop(0, rows // 16, group, 0)
    for i in range(rows // 16):
        to = query.at[pl.ds(16 * i, 16)] if 16 * i < split else gate.at[pl.ds(16 * i - split, 16)]
        copies.append(pltpu.make_async_copy(tiles.at[pl.ds(16 * i, 16)], to, sems.at[i]))
    for copy in copies:
        copy.wait()


def on_device(grad_query, grad_gate, old_master, old_moment, old_variance, old_bounds, stop=9):
    query_rows, row_width = grad_query.shape[1:]
    gate_rows = grad_gate.shape[1]
    query = grad_query.reshape(query_rows, row_width)
    gate = grad_gate.reshape(gate_rows, row_width)
    old = [a.reshape(-1, LANE) for a in (old_master, old_moment, old_variance)]
    query, gate, *old, old_bounds = [
        pltpu.with_memory_space_constraint(a, pltpu.HBM) for a in (query, gate, *old, old_bounds)
    ]
    hbm = pl.BlockSpec(memory_space=pltpu.HBM)
    vmem = pl.BlockSpec(memory_space=pltpu.VMEM)
    dma = pltpu.SemaphoreType.DMA
    shard = jax.ShapeDtypeStruct((96, LANE), F32)
    rows = query_rows + gate_rows
    new_m, new_v, new_s, weights = pl.pallas_call(
        functools.partial(kernel, stop),
        out_shape=(
            pltpu.VMEM(shard.shape, F32), pltpu.VMEM(shard.shape, F32), pltpu.VMEM(shard.shape, F32),
            pltpu.VMEM((4, 4, 4, 6, BLK, LANE), BF16),
        ),
        in_specs=[hbm] * 6,
        out_specs=(vmem, vmem, vmem, vmem),
        scratch_shapes=[
            pltpu.VMEM((rows, row_width // 2), BF16),
            pltpu.VMEM((rows, row_width // 2), BF16),
            pltpu.VMEM((rows, PITCH, LANE), F32),
            pltpu.VMEM((3, 4, 4, 4, BLK, LANE), jnp.int16),
            pltpu.VMEM((3, 3, 4, 4, BLK, LANE), jnp.int16),
            pltpu.VMEM((3, 16, BLK, LANE), F32),
            pltpu.VMEM((3, 16, BLK, LANE), jnp.int16),
            pltpu.VMEM((3, 3, 4, BLK, LANE), jnp.int16),
            pltpu.VMEM((3, 4, BLK, LANE), F32),
            pltpu.VMEM((3, 4, BLK, LANE), F32),
            pltpu.VMEM((3, 368, LANE), F32),
            pltpu.VMEM((3, 96, LANE), F32),
            pltpu.VMEM((3, 96, LANE), F32),
            pltpu.SMEM((1, 2), jnp.int32),
            dma((9,)),
            dma((5,)), dma((5,)),
            dma((27,)), dma((27,)),
            dma((9,)), dma((9,)),
            dma((12,)), dma((12,)),
            dma((1,)), dma((1,)),
            dma((54,)), dma((54,)),
            dma((12,)), dma((12,)),
            dma((1,)), dma((1,)),
        ],
        compiler_params=pltpu.CompilerParams(
            collective_id=0, has_side_effects=True, vmem_limit_bytes=48 * 1024 * 1024
        ),
    )(query, gate, *old, old_bounds)
    query_new, gate_new, new_m, new_v, new_s = pl.pallas_call(
        write,
        out_shape=(
            jax.ShapeDtypeStruct((query_rows, row_width), BF16),
            jax.ShapeDtypeStruct((gate_rows, row_width), BF16),
            shard, shard, shard,
        ),
        in_specs=[vmem] * 4,
        out_specs=(hbm,) * 5,
        scratch_shapes=[pltpu.VMEM((rows, row_width), BF16), dma((rows // 16 + 3,))],
        compiler_params=pltpu.CompilerParams(vmem_limit_bytes=48 * 1024 * 1024),
    )(weights.reshape(rows, row_width // LANE, LANE), new_m, new_v, new_s)
    return (new_m.reshape(-1), new_v.reshape(-1), new_s.reshape(-1), query_new, gate_new)


def solution(mesh, stop=9):
    placed = (P("dp", None, None), P("dp", None, None), P("dp"), P("dp"), P("dp"), P("dp", None))
    return jax.shard_map(
        functools.partial(on_device, stop=stop),
        mesh=mesh,
        in_specs=placed,
        out_specs=(P("dp"), P("dp"), P("dp"), P(), P()),
        check_vma=False,
    )
```

```python
import functools

import jax
import jax.numpy as jnp
from jax import lax
from jax.experimental import pallas as pl
from jax.experimental.pallas import tpu as pltpu
from jax.sharding import PartitionSpec as P

MESH = pl.DeviceIdType.MESH
F32 = jnp.float32
BF16 = jnp.bfloat16

STEP = 10
beta_one = 0.9
beta_two = 0.95
learn_rate = 0.01
decay_rate = 0.1
epsilon = 1e-08

LANE = 128
BLK = 32
HALF = 16
PITCH = 24
BOUND = (48.0, 192.0)
TURNS = (0, 1, 3, 2)
AWAY = ((2, 2), (2, 1), (1, 2), (2, -1), (-1, 2), (1, 1), (1, -1), (-1, 1), (-1, -1),
        (2, 0), (0, 2), (1, 0), (0, 1), (-1, 0), (0, -1))
ORDER = ((0, 1, 2), (1, 2, 0), (2, 0, 1))


def adamw_step(master, moment, variance, grad):
    moment_new = beta_one * moment + (1.0 - beta_one) * grad
    variance_new = beta_two * variance + (1.0 - beta_two) * grad * grad
    corrected_m = moment_new / (1.0 - beta_one**STEP)
    corrected_v = variance_new / (1.0 - beta_two**STEP)
    master_new = master - learn_rate * (
        corrected_m / (jnp.sqrt(corrected_v) + epsilon) + decay_rate * master
    )
    return (master_new, moment_new, variance_new)


def encode(value, bound):
    ratio = jnp.maximum(jnp.abs(value), 1e-30) * (1.0 / bound)
    root = lax.rsqrt(lax.rsqrt(ratio))
    code = root * lax.rsqrt(root) * 32767.0
    return jnp.round(jnp.where(value < 0, -code, code)).astype(jnp.int32).astype(jnp.int16)


def decode(code, bound):
    root = code.astype(jnp.int32).astype(F32) * (bound**0.125 / 32767.0)
    square = root * root
    return (root * jnp.abs(root)) * (square * (square * square))


def kernel(
    stop,
    query, gate, old_m, old_v, old_s, bounds_hbm,
    new_m, new_v, new_s, weights,
    mine, other, s0, e0, r0, s1, e1, r1, state, passed, arrived, bounds,
    load_sem, near_sem, send_sem, s0_recv, s1_recv, s2_recv, g1_recv, g2_recv, g3_recv, c_recv, p_recv,
):
    me = lax.axis_index("dp")
    core = me % 2
    chip = me // 2
    at = (chip // 16, (chip // 4) % 4, chip % 4)
    sibling = me + 1 - 2 * core

    def device(moves, on_core):
        place = [(at[axis] + moves.get(axis, 0)) % 4 for axis in range(3)]
        return ((place[0] * 4 + place[1]) * 4 + place[2]) * 2 + on_core

    def remote(src, dst, send, recv, to):
        return pltpu.make_async_remote_copy(
            src_ref=src, dst_ref=dst, send_sem=send, recv_sem=recv,
            device_id=(to,), device_id_type=MESH,
        )

    over = []

    def start(src, dst, send, recv, to):
        remote(src, dst, send_sem.at[send], recv, to).start()

    def await_from(dst, recv):
        remote(dst, dst, send_sem.at[0], recv, sibling).wait_recv()

    def done():
        totals = (
            other, e0.at[:, :, pl.ds(0, 3)], e1.at[:, pl.ds(0, 15)],
            weights.at[0, 0, pl.ds(0, 3), pl.ds(0, 3)], weights.at[0, pl.ds(0, 3), :, pl.ds(0, 3)],
            weights.at[pl.ds(0, 3), :, :, pl.ds(0, 3)], weights.at[:, :, :, pl.ds(0, 3)],
        )
        for n in range({0: 1, 1: 2, 3: 3}.get(stop, 7)):
            remote(totals[n], totals[n], send_sem.at[n], s0_recv.at[0], sibling).wait_send()
        for crosses, across in over:
            @pl.when(crosses)
            def _(across=across):
                across.wait_send()

        @pl.when(hands_on)
        def _():
            handed.wait_send()

        if 0 <= stop < 3:
            @pl.when(takes)
            def _():
                handed.wait_recv()

    wide = mine.shape[2]
    split = query.shape[0]
    loads, olds, swaps = [], [], []
    for g in range(2):
        own_half = pl.ds(pl.multiple_of((2 * core + g) * wide, wide), wide)
        its_half = pl.ds(pl.multiple_of((2 - 2 * core + g) * wide, wide), wide)
        for n, (array, rows) in enumerate(((query, pl.ds(0, split)), (gate, pl.ds(split, gate.shape[0])))):
            loads.append(pltpu.make_async_copy(
                array.at[:, own_half], mine.at[g, rows], load_sem.at[g]))
            swaps.append(remote(
                array.at[:, its_half], other.at[g, rows], send_sem.at[0], s0_recv.at[g], sibling))
    for n, old in enumerate((old_m, old_v, old_s)):
        olds.append(
            pltpu.make_async_copy(old, state.at[n, pl.ds(96, 176)], load_sem.at[2])
        )
    olds.append(pltpu.make_async_copy(bounds_hbm, bounds, load_sem.at[3]))
    for copy in olds + loads:
        copy.start()

    barrier = pltpu.get_barrier_semaphore()
    around = [sibling] + [device({axis: by}, core) for axis in range(3) for by in (1, 3)]

    def greet(sem):
        for to in around:
            pl.semaphore_signal(sem, inc=1, device_id=(to,), device_id_type=MESH)

    greet(barrier)

    for n in range(3):
        state[n, pl.ds(0, 96)] = jnp.zeros((96, LANE), F32)
        state[n, pl.ds(272, 96)] = jnp.zeros((96, LANE), F32)
    olds[-1].wait()
    whole = state.at[:, pl.ds(96, 176)]
    pltpu.make_async_copy(whole, whole, load_sem.at[2]).wait()
    first = bounds[0, 0] // LANE
    last = bounds[0, 1] // LANE

    def window(n, base):
        rows = lax.broadcasted_iota(jnp.int32, (96, LANE), 0) + base
        piece = state[n, pl.ds(jnp.clip(base - first + 96, 0, 272), 96)]
        return jnp.where((rows >= first) & (rows < last), piece, 0.0)

    for n in range(3):
        passed[n] = window(n, (me + 1) * 96)
    for n, ref in enumerate((new_m, new_v, new_s)):
        ref[...] = window(n, me * 96)

    pl.semaphore_wait(barrier, len(around))

    for copy in swaps:
        copy.start()
    greet(near_sem.at[0])

    hands_on = (core == 0) | (at[2] % 2 == 0)
    takes = (core == 1) | (at[2] % 2 == 1)
    handed = remote(
        passed, arrived, send_sem.at[7], p_recv.at[0],
        sibling * (1 - core) + device({2: 1}, 0) * core,
    )

    def round_of(n):
        pl.semaphore_wait(near_sem.at[n], len(around))
        if n < 3:
            greet(near_sem.at[n + 1])

    flat0 = s0.reshape(2 * 192 * PITCH, LANE)
    blocks0 = s0.reshape(2, 4, 4, 4, 3, PITCH, LANE)
    rows0 = pl.ds(0, HALF)

    def block(p, g, a, b, c):
        place = [None] * 3
        for axis, value in zip(ORDER[p], (a, b, c)):
            place[axis] = value
        return blocks0[g, place[0], place[1], place[2], p, rows0]

    def slab_out(p, g, by):
        a = (at[ORDER[p][0]] + by) % 4

        def code(b, carry):
            for c in range(4):
                e0[p, g, a, b, c] = encode(block(p, g, a, b, c), BOUND[0])
            return carry

        lax.fori_loop(0, 4, code, 0)
        start(
            e0.at[p, g, a], r0.at[p, g, by - 1], 1, s1_recv.at[(p * 2 + g) * 3 + by - 1],
            device({ORDER[p][0]: by}, core),
        )

    for g in range(2):
        pltpu.make_async_copy(mine.at[g], mine.at[g], load_sem.at[g]).wait()
        await_from(other.at[g], s0_recv.at[g])

        def pair(i, carry, g=g):
            row = pl.multiple_of(16 * i, 16)
            for j in range(HALF):
                lanes = pl.ds(j * LANE, LANE)
                both = mine[g, pl.ds(row, 16), lanes].astype(F32) + other[g, pl.ds(row, 16), lanes].astype(F32)
                flat0[pl.ds((g * 192 + row) * PITCH + j, 16, stride=PITCH), :] = both
            return carry

        lax.fori_loop(0, 12, pair, 0)
        for by in (1, 3, 2):
            if by == 2:
                round_of(g)
            for p in range(3):
                if stop != 0:
                    slab_out(p, g, by)
        if g == 0:
            @pl.when(hands_on)
            def _():
                handed.start()
    round_of(2)
    if stop == 0:
        round_of(3)
        return done()

    for g in range(2):
        for p in range(3):
            for by in (1, 3):
                await_from(r0.at[p, g, by - 1], s1_recv.at[(p * 2 + g) * 3 + by - 1])

            def gather_one(b, carry, p=p, g=g):
                for c in range(4):
                    s1[p, b, c] = block(p, g, at[ORDER[p][0]], b, c) + (
                        decode(r0[p, g, 0, b, c], BOUND[0]) + decode(r0[p, g, 2, b, c], BOUND[0]))
                return carry

            lax.fori_loop(0, 4, gather_one, 0)
        if g == 1:
            round_of(3)
        for p in range(3):
            await_from(r0.at[p, g, 1], s1_recv.at[(p * 2 + g) * 3 + 1])

            def gather_two(b, carry, p=p, g=g):
                for c in range(4):
                    total = s1[p, b, c] + decode(r0[p, g, 1, b, c], BOUND[0])
                    e1[p, b * 4 + c, pl.ds(g * HALF, HALF)] = encode(total, BOUND[1])
                return carry

            lax.fori_loop(0, 4, gather_two, 0)
            if g == 0 or stop == 1:
                continue
            _, b, c = ORDER[p]
            unit = 2 * p + core
            owner = unit // 3
            place = unit % 3
            source = at[b] * 4 + at[c]
            for db, dc in AWAY:
                start(
                    e1.at[p, (at[b] + db) % 4 * 4 + (at[c] + dc) % 4], r1.at[place, source],
                    2, s2_recv.at[place], device({b: db, c: dc}, owner),
                )
            if p == 1:
                r1[place, source] = e1[p, source]
            else:
                across = remote(
                    e1.at[p, source], r1.at[place, source], send_sem.at[8], s2_recv.at[place], sibling,
                )
                crosses = core == (1 if p == 0 else 0)

                @pl.when(crosses)
                def _(across=across):
                    across.start()

                over.append((crosses, across))

                @pl.when(jnp.logical_not(crosses))
                def _(p=p, place=place, source=source):
                    r1[place, source] = e1[p, source]
    if stop == 1:
        return done()

    @pl.when(takes)
    def _():
        handed.wait_recv()

    @pl.when(jnp.logical_not(takes))
    def _():
        arrived[...] = jnp.zeros_like(arrived)

    for n, ref in enumerate((new_m, new_v, new_s)):
        ref[...] += arrived[n]

    for m in range(3):
        await_from(r1.at[m, pl.ds(0, 16 if m == 1 else 15)], s2_recv.at[m])
        values = [decode(r1[m, n], BOUND[1]) for n in range(16)]
        while len(values) > 1:
            values = [one + two for one, two in zip(values[::2], values[1::2])]
        total = values[0]
        rows = pl.ds(m * BLK, BLK)
        master, moment, variance = adamw_step(new_m[rows], new_v[rows], new_s[rows], total)
        new_m[rows] = master
        new_v[rows] = moment
        new_s[rows] = variance
        weights[at[0], at[1], at[2], 3 * core + m] = master.astype(BF16)
        if stop == 3:
            continue
        _, b, c = ORDER[m]
        own = weights.at[at[0], at[1], at[2], 3 * core + m]
        for by in (2, 1, 3):
            start(own, own, 3, g1_recv.at[m], device({c: by}, core))
    if stop == 3:
        return done()

    def slab(m, moves, free, on_core):
        index = [(at[axis] + moves.get(axis, 0)) % 4 for axis in range(3)]
        for axis in free:
            index[axis] = slice(None)
        return weights.at[index[0], index[1], index[2], 3 * on_core + m]

    def forward(m, moves, free):
        part = slab(m, moves, free, core)
        start(part, part, 6, c_recv.at[0], sibling)

    def group_out(m, turn):
        a, b, c = ORDER[m]
        part = slab(m, {b: -TURNS[turn]}, (c,), core)
        for by in (2, 1, 3):
            start(
                part, part, 5, g3_recv.at[m * 6 + (by - 1) * 2 + turn // 2], device({a: by}, core)
            )

    for m in range(3):
        a, b, c = ORDER[m]
        await_from(weights.at[0, 0, pl.ds(0, 3), m], g1_recv.at[m])
        part = slab(m, {}, (c,), core)
        for by in (2, 1, 3):
            start(part, part, 4, g2_recv.at[m * 3 + by - 1], device({b: by}, core))
        group_out(m, 0)
    for turn in (1, 2, 3):
        for m in range(3):
            a, b, c = ORDER[m]
            by = TURNS[turn]
            await_from(slab(m, {b: -by}, (c,), core), g2_recv.at[m * 3 + by - 1])
            group_out(m, turn)
    for m in range(3):
        forward(m, {}, ORDER[m][1:])
    for part in range(2):
        for by in (1, 3, 2):
            for m in range(3):
                a, b, c = ORDER[m]
                await_from(weights.at[0, pl.ds(0, 2), :, m], g3_recv.at[m * 6 + (by - 1) * 2 + part])
                for turn in (2 * part, 2 * part + 1):
                    forward(m, {a: -by, b: -TURNS[turn]}, (c,))
    await_from(weights.at[:, :, :, pl.ds(0, 3)], c_recv.at[0])
    done()


def write(weights, new_m, new_v, new_s, query, gate, out_m, out_v, out_s, tiles, sems):
    split, rows = query.shape[0], tiles.shape[0]
    copies = [
        pltpu.make_async_copy(src, dst, sems.at[rows // 16 + n])
        for n, (src, dst) in enumerate(((new_m, out_m), (new_v, out_v), (new_s, out_s)))
    ]

    def group(i, carry):
        at = pl.ds(pl.multiple_of(16 * i, 16), 16)
        for j in range(0, weights.shape[1], 8):
            block = jnp.swapaxes(weights[at, pl.ds(j, 8)], 0, 1)
            for k in range(8):
                tiles[at, pl.ds((j + k) * LANE, LANE)] = block[k]

        @pl.when(i < split // 16)
        def _():
            pltpu.make_async_copy(tiles.at[at], query.at[at], sems.at[i]).start()

        @pl.when(i >= split // 16)
        def _():
            to = pl.ds(pl.multiple_of(16 * i - split, 16), 16)
            pltpu.make_async_copy(tiles.at[at], gate.at[to], sems.at[i]).start()

        return carry

    for copy in copies:
        copy.start()
    lax.fori_loop(0, rows // 16, group, 0)
    for i in range(rows // 16):
        to = query.at[pl.ds(16 * i, 16)] if 16 * i < split else gate.at[pl.ds(16 * i - split, 16)]
        copies.append(pltpu.make_async_copy(tiles.at[pl.ds(16 * i, 16)], to, sems.at[i]))
    for copy in copies:
        copy.wait()


def on_device(grad_query, grad_gate, old_master, old_moment, old_variance, old_bounds, stop=9):
    query_rows, row_width = grad_query.shape[1:]
    gate_rows = grad_gate.shape[1]
    query = grad_query.reshape(query_rows, row_width)
    gate = grad_gate.reshape(gate_rows, row_width)
    old = [a.reshape(-1, LANE) for a in (old_master, old_moment, old_variance)]
    query, gate, *old, old_bounds = [
        pltpu.with_memory_space_constraint(a, pltpu.HBM) for a in (query, gate, *old, old_bounds)
    ]
    hbm = pl.BlockSpec(memory_space=pltpu.HBM)
    vmem = pl.BlockSpec(memory_space=pltpu.VMEM)
    dma = pltpu.SemaphoreType.DMA
    shard = jax.ShapeDtypeStruct((96, LANE), F32)
    rows = query_rows + gate_rows
    new_m, new_v, new_s, weights = pl.pallas_call(
        functools.partial(kernel, stop),
        out_shape=(
            pltpu.VMEM(shard.shape, F32), pltpu.VMEM(shard.shape, F32), pltpu.VMEM(shard.shape, F32),
            pltpu.VMEM((4, 4, 4, 6, BLK, LANE), BF16),
        ),
        in_specs=[hbm] * 6,
        out_specs=(vmem, vmem, vmem, vmem),
        scratch_shapes=[
            pltpu.VMEM((2, rows, row_width // 4), BF16),
            pltpu.VMEM((2, rows, row_width // 4), BF16),
            pltpu.VMEM((2, rows, PITCH, LANE), F32),
            pltpu.VMEM((3, 2, 4, 4, 4, HALF, LANE), jnp.int16),
            pltpu.VMEM((3, 2, 3, 4, 4, HALF, LANE), jnp.int16),
            pltpu.VMEM((3, 4, 4, HALF, LANE), F32),
            pltpu.VMEM((3, 16, BLK, LANE), jnp.int16),
            pltpu.VMEM((3, 16, BLK, LANE), jnp.int16),
            pltpu.VMEM((3, 368, LANE), F32),
            pltpu.VMEM((3, 96, LANE), F32),
            pltpu.VMEM((3, 96, LANE), F32),
            pltpu.SMEM((1, 2), jnp.int32),
            dma((4,)),
            pltpu.SemaphoreType.REGULAR((4,)),
            dma((9,)),
            dma((2,)), dma((18,)), dma((3,)),
            dma((3,)), dma((9,)), dma((18,)), dma((1,)), dma((1,)),
        ],
        compiler_params=pltpu.CompilerParams(
            collective_id=0, has_side_effects=True, vmem_limit_bytes=48 * 1024 * 1024
        ),
    )(query, gate, *old, old_bounds)
    query_new, gate_new, new_m, new_v, new_s = pl.pallas_call(
        write,
        out_shape=(
            jax.ShapeDtypeStruct((query_rows, row_width), BF16),
            jax.ShapeDtypeStruct((gate_rows, row_width), BF16),
            shard, shard, shard,
        ),
        in_specs=[vmem] * 4,
        out_specs=(hbm,) * 5,
        scratch_shapes=[pltpu.VMEM((rows, row_width), BF16), dma((rows // 16 + 3,))],
        compiler_params=pltpu.CompilerParams(vmem_limit_bytes=48 * 1024 * 1024),
    )(weights.reshape(rows, row_width // LANE, LANE), new_m, new_v, new_s)
    return (new_m.reshape(-1), new_v.reshape(-1), new_s.reshape(-1), query_new, gate_new)


def solution(mesh, stop=9):
    placed = (P("dp", None, None), P("dp", None, None), P("dp"), P("dp"), P("dp"), P("dp", None))
    return jax.shard_map(
        functools.partial(on_device, stop=stop),
        mesh=mesh,
        in_specs=placed,
        out_specs=(P("dp"), P("dp"), P("dp"), P(), P()),
        check_vma=False,
    )
```

```python
import functools

import jax
import jax.numpy as jnp
from jax import lax
from jax.experimental import pallas as pl
from jax.experimental.pallas import tpu as pltpu
from jax.sharding import PartitionSpec as P

MESH = pl.DeviceIdType.MESH
F32 = jnp.float32
BF16 = jnp.bfloat16

STEP = 10
beta_one = 0.9
beta_two = 0.95
learn_rate = 0.01
decay_rate = 0.1
epsilon = 1e-08

LANE = 128
BLK = 32
HALF = 16
PITCH = 24
BOUND = (48.0, 192.0)
AWAY = ((2, 2), (2, 1), (1, 2), (2, -1), (-1, 2), (1, 1), (1, -1), (-1, 1), (-1, -1),
        (2, 0), (0, 2), (1, 0), (0, 1), (-1, 0), (0, -1))
ORDER = ((0, 1, 2), (1, 2, 0), (2, 0, 1))


def adamw_step(master, moment, variance, grad):
    moment_new = beta_one * moment + (1.0 - beta_one) * grad
    variance_new = beta_two * variance + (1.0 - beta_two) * grad * grad
    corrected_m = moment_new / (1.0 - beta_one**STEP)
    corrected_v = variance_new / (1.0 - beta_two**STEP)
    master_new = master - learn_rate * (
        corrected_m / (jnp.sqrt(corrected_v) + epsilon) + decay_rate * master
    )
    return (master_new, moment_new, variance_new)


def encode(value, bound):
    ratio = jnp.maximum(jnp.abs(value), 1e-30) * (1.0 / bound)
    root = lax.rsqrt(lax.rsqrt(ratio))
    code = root * lax.rsqrt(root) * 32767.0
    return jnp.round(jnp.where(value < 0, -code, code)).astype(jnp.int32).astype(jnp.int16)


def decode(code, bound):
    root = code.astype(jnp.int32).astype(F32) * (bound**0.125 / 32767.0)
    square = root * root
    return (root * jnp.abs(root)) * (square * (square * square))


def kernel(
    stop,
    query, gate, old_m, old_v, old_s, bounds_hbm,
    new_m, new_v, new_s, weights,
    mine, other, s0, e0, r0, s1, e1, r1, state, passed, arrived, bounds,
    load_sem, near_sem, send_sem, s0_recv, s1_recv, s2_recv, g1_recv, g2_recv, g3_recv, c_recv, p_recv,
):
    me = lax.axis_index("dp")
    core = me % 2
    chip = me // 2
    at = (chip // 16, (chip // 4) % 4, chip % 4)
    sibling = me + 1 - 2 * core

    def device(moves, on_core):
        place = [(at[axis] + moves.get(axis, 0)) % 4 for axis in range(3)]
        return ((place[0] * 4 + place[1]) * 4 + place[2]) * 2 + on_core

    def remote(src, dst, send, recv, to):
        return pltpu.make_async_remote_copy(
            src_ref=src, dst_ref=dst, send_sem=send, recv_sem=recv,
            device_id=(to,), device_id_type=MESH,
        )

    def start(src, dst, send, recv, to):
        remote(src, dst, send_sem.at[send], recv, to).start()

    def await_from(dst, recv):
        remote(dst, dst, send_sem.at[0], recv, sibling).wait_recv()

    def done():
        totals = (
            other, e0.at[:, :, pl.ds(0, 3)], e1.at[:, :, pl.ds(0, 15)],
            weights.at[0, :, :, 0, 0, pl.ds(0, 3)], weights.at[0, :, :, 0, pl.ds(0, 3)],
            weights.at[0, :, :, pl.ds(0, 3)], weights.at[0],
        )
        for n in range({0: 1, 1: 2, 3: 3}.get(stop, 7)):
            remote(totals[n], totals[n], send_sem.at[n], s0_recv.at[0], sibling).wait_send()
        if stop > 1:
            for p, on_core in ((0, 1), (2, 0)):
                @pl.when(core == on_core)
                def _(p=p):
                    remote(e1.at[p, :, 0], e1.at[p, :, 0], send_sem.at[8], s0_recv.at[0], sibling).wait_send()

        @pl.when(hands_on)
        def _():
            handed.wait_send()

        if 0 <= stop < 3:
            @pl.when(takes)
            def _():
                handed.wait_recv()

    wide = mine.shape[2]
    split = query.shape[0]
    loads, olds, swaps = [], [], []
    for g in range(2):
        own_half = pl.ds(pl.multiple_of((2 * core + g) * wide, wide), wide)
        its_half = pl.ds(pl.multiple_of((2 - 2 * core + g) * wide, wide), wide)
        for n, (array, rows) in enumerate(((query, pl.ds(0, split)), (gate, pl.ds(split, gate.shape[0])))):
            loads.append(pltpu.make_async_copy(
                array.at[:, own_half], mine.at[g, rows], load_sem.at[g]))
            swaps.append(remote(
                array.at[:, its_half], other.at[g, rows], send_sem.at[0], s0_recv.at[g], sibling))
    for n, old in enumerate((old_m, old_v, old_s)):
        olds.append(
            pltpu.make_async_copy(old, state.at[n, pl.ds(96, 176)], load_sem.at[2])
        )
    olds.append(pltpu.make_async_copy(bounds_hbm, bounds, load_sem.at[3]))
    for copy in olds + loads:
        copy.start()

    barrier = pltpu.get_barrier_semaphore()
    around = [sibling] + [device({axis: by}, core) for axis in range(3) for by in (1, 3)]

    def greet(sem):
        for to in around:
            pl.semaphore_signal(sem, inc=1, device_id=(to,), device_id_type=MESH)

    greet(barrier)

    for n in range(3):
        state[n, pl.ds(0, 96)] = jnp.zeros((96, LANE), F32)
        state[n, pl.ds(272, 96)] = jnp.zeros((96, LANE), F32)
    olds[-1].wait()
    whole = state.at[:, pl.ds(96, 176)]
    pltpu.make_async_copy(whole, whole, load_sem.at[2]).wait()
    first = bounds[0, 0] // LANE
    last = bounds[0, 1] // LANE

    def window(n, base):
        rows = lax.broadcasted_iota(jnp.int32, (96, LANE), 0) + base
        piece = state[n, pl.ds(jnp.clip(base - first + 96, 0, 272), 96)]
        return jnp.where((rows >= first) & (rows < last), piece, 0.0)

    for n in range(3):
        passed[n] = window(n, (me + 1) * 96)
    for n, ref in enumerate((new_m, new_v, new_s)):
        ref[...] = window(n, me * 96)

    pl.semaphore_wait(barrier, len(around))

    for copy in swaps:
        copy.start()
    greet(near_sem.at[0])

    hands_on = (core == 0) | (at[2] % 2 == 0)
    takes = (core == 1) | (at[2] % 2 == 1)
    handed = remote(
        passed, arrived, send_sem.at[7], p_recv.at[0],
        sibling * (1 - core) + device({2: 1}, 0) * core,
    )

    def round_of(n):
        pl.semaphore_wait(near_sem.at[n], len(around))
        if n < 3:
            greet(near_sem.at[n + 1])

    flat0 = s0.reshape(2 * 192 * PITCH, LANE)
    blocks0 = s0.reshape(2, 4, 4, 4, 3, PITCH, LANE)
    rows0 = pl.ds(0, HALF)

    def block(p, g, a, b, c):
        place = [None] * 3
        for axis, value in zip(ORDER[p], (a, b, c)):
            place[axis] = value
        return blocks0[g, place[0], place[1], place[2], p, rows0]

    def slab_out(p, g, by):
        a = (at[ORDER[p][0]] + by) % 4

        def code(b, carry):
            for c in range(4):
                e0[p, g, a, b, c] = encode(block(p, g, a, b, c), BOUND[0])
            return carry

        lax.fori_loop(0, 4, code, 0)
        start(
            e0.at[p, g, a], r0.at[p, g, by - 1], 1, s1_recv.at[(p * 2 + g) * 3 + by - 1],
            device({ORDER[p][0]: by}, core),
        )

    for g in range(2):
        pltpu.make_async_copy(mine.at[g], mine.at[g], load_sem.at[g]).wait()
        await_from(other.at[g], s0_recv.at[g])

        def pair(i, carry, g=g):
            row = pl.multiple_of(16 * i, 16)
            for j in range(HALF):
                lanes = pl.ds(j * LANE, LANE)
                both = mine[g, pl.ds(row, 16), lanes].astype(F32) + other[g, pl.ds(row, 16), lanes].astype(F32)
                flat0[pl.ds((g * 192 + row) * PITCH + j, 16, stride=PITCH), :] = both
            return carry

        lax.fori_loop(0, 12, pair, 0)
        for by in (1, 3, 2):
            if by == 2:
                round_of(g)
            for p in range(3):
                if stop != 0:
                    slab_out(p, g, by)
        if g == 0:
            @pl.when(hands_on)
            def _():
                handed.start()
    round_of(2)
    if stop == 0:
        round_of(3)
        return done()

    def plane_out(g):
        for p in range(3):
            for by in (1, 3):
                await_from(r0.at[p, g, by - 1], s1_recv.at[(p * 2 + g) * 3 + by - 1])

            def gather_one(b, carry, p=p):
                for c in range(4):
                    s1[p, b, c] = block(p, g, at[ORDER[p][0]], b, c) + (
                        decode(r0[p, g, 0, b, c], BOUND[0]) + decode(r0[p, g, 2, b, c], BOUND[0]))
                return carry

            lax.fori_loop(0, 4, gather_one, 0)
        if g == 0:
            round_of(3)
        for p in range(3):
            await_from(r0.at[p, g, 1], s1_recv.at[(p * 2 + g) * 3 + 1])

            def gather_two(b, carry, p=p):
                for c in range(4):
                    total = s1[p, b, c] + decode(r0[p, g, 1, b, c], BOUND[0])
                    e1[p, g, b * 4 + c] = encode(total, BOUND[1])
                return carry

            lax.fori_loop(0, 4, gather_two, 0)
            if stop == 1:
                continue
            _, b, c = ORDER[p]
            unit = 2 * p + core
            owner = unit // 3
            place = unit % 3
            source = at[b] * 4 + at[c]
            for db, dc in AWAY:
                start(
                    e1.at[p, g, (at[b] + db) % 4 * 4 + (at[c] + dc) % 4], r1.at[g, place, source],
                    2, s2_recv.at[g * 3 + place], device({b: db, c: dc}, owner),
                )
            if p == 1:
                r1[g, place, source] = e1[p, g, source]
            else:
                crosses = core == (1 if p == 0 else 0)

                @pl.when(crosses)
                def _(p=p, place=place, source=source):
                    start(
                        e1.at[p, g, source], r1.at[g, place, source],
                        8, s2_recv.at[g * 3 + place], sibling,
                    )

                @pl.when(jnp.logical_not(crosses))
                def _(p=p, place=place, source=source):
                    r1[g, place, source] = e1[p, g, source]

    def group(m, g, da, db):
        a, b, _ = ORDER[m]
        return weights.at[core, g, m, (at[a] + da) % 4, (at[b] + db) % 4]

    def step(g):
        for m in range(3):
            await_from(r1.at[g, m, pl.ds(0, 16 if m == 1 else 15)], s2_recv.at[g * 3 + m])
            values = [decode(r1[g, m, n], BOUND[1]) for n in range(16)]
            while len(values) > 1:
                values = [one + two for one, two in zip(values[::2], values[1::2])]
            rows = pl.ds(m * BLK + g * HALF, HALF)
            master, moment, variance = adamw_step(new_m[rows], new_v[rows], new_s[rows], values[0])
            new_m[rows] = master
            new_v[rows] = moment
            new_s[rows] = variance
            own = weights.at[(core, g, m) + tuple(at[axis] for axis in ORDER[m])]
            own[...] = master.astype(BF16)
            if stop == 3:
                continue
            for by in (2, 1, 3):
                start(own, own, 3, g1_recv.at[g * 3 + m], device({ORDER[m][2]: by}, core))

    def group_out(m, g, db):
        part = group(m, g, 0, -db)
        for by in (2, 1, 3):
            start(part, part, 5, g3_recv.at[(g * 3 + m) * 3 + by - 1], device({ORDER[m][0]: by}, core))

    def second_level(g):
        for m in range(3):
            await_from(weights.at[0, g, m, 0, 0, pl.ds(0, 3)], g1_recv.at[g * 3 + m])
            part = group(m, g, 0, 0)
            for by in (2, 1, 3):
                start(part, part, 4, g2_recv.at[(g * 3 + m) * 3 + by - 1], device({ORDER[m][1]: by}, core))
        for m in range(3):
            group_out(m, g, 0)

    def third_level(g):
        for by in (1, 3, 2):
            for m in range(3):
                await_from(group(m, g, 0, -by), g2_recv.at[(g * 3 + m) * 3 + by - 1])
                group_out(m, g, by)

    def forward(g):
        for by in (0, 1, 3, 2):
            for m in range(3):
                part = weights.at[core, g, m, (at[ORDER[m][0]] - by) % 4]
                if by:
                    await_from(part, g3_recv.at[(g * 3 + m) * 3 + by - 1])
                start(part, part, 6, c_recv.at[0], sibling)

    for g in range(2):
        plane_out(g)
    if stop == 1:
        return done()

    @pl.when(takes)
    def _():
        handed.wait_recv()

    @pl.when(jnp.logical_not(takes))
    def _():
        arrived[...] = jnp.zeros_like(arrived)

    for n, ref in enumerate((new_m, new_v, new_s)):
        ref[...] += arrived[n]

    for g in range(2):
        step(g)
    if stop == 3:
        return done()
    for stage in (second_level, third_level, forward):
        for g in range(2):
            stage(g)
    await_from(weights.at[0], c_recv.at[0])
    done()


def write(weights, new_m, new_v, new_s, query, gate, out_m, out_v, out_s, tiles, sems):
    split, rows = query.shape[0], tiles.shape[0]
    copies = [
        pltpu.make_async_copy(src, dst, sems.at[rows // 16 + n])
        for n, (src, dst) in enumerate(((new_m, out_m), (new_v, out_v), (new_s, out_s)))
    ]

    def rows_of(x, third):
        i = 3 * x + third
        at = pl.ds(pl.multiple_of(16 * i, 16), 16)
        for j in range(0, 2 * BLK, 8):
            picked = []
            for row in range(16 * third, 16 * third + 16):
                chip = (x, row // 12, row // 3 % 4)
                unit = row % 3 * 2 + j // BLK
                m = unit % 3
                place = (unit // 3, j % BLK // HALF, m) + tuple(chip[axis] for axis in ORDER[m])
                picked.append(weights[place + (pl.ds(j % HALF, 8),)])
            block = jnp.swapaxes(jnp.stack(picked), 0, 1)
            for k in range(8):
                tiles[at, pl.ds((j + k) * LANE, LANE)] = block[k]

        @pl.when(i < split // 16)
        def _():
            pltpu.make_async_copy(tiles.at[at], query.at[at], sems.at[i]).start()

        @pl.when(i >= split // 16)
        def _():
            to = pl.ds(pl.multiple_of(16 * i - split, 16), 16)
            pltpu.make_async_copy(tiles.at[at], gate.at[to], sems.at[i]).start()

    def plane(x, carry):
        for third in range(3):
            rows_of(x, third)
        return carry

    for copy in copies:
        copy.start()
    lax.fori_loop(0, 4, plane, 0)
    for i in range(rows // 16):
        to = query.at[pl.ds(16 * i, 16)] if 16 * i < split else gate.at[pl.ds(16 * i - split, 16)]
        copies.append(pltpu.make_async_copy(tiles.at[pl.ds(16 * i, 16)], to, sems.at[i]))
    for copy in copies:
        copy.wait()


def on_device(grad_query, grad_gate, old_master, old_moment, old_variance, old_bounds, stop=9):
    query_rows, row_width = grad_query.shape[1:]
    gate_rows = grad_gate.shape[1]
    query = grad_query.reshape(query_rows, row_width)
    gate = grad_gate.reshape(gate_rows, row_width)
    old = [a.reshape(-1, LANE) for a in (old_master, old_moment, old_variance)]
    query, gate, *old, old_bounds = [
        pltpu.with_memory_space_constraint(a, pltpu.HBM) for a in (query, gate, *old, old_bounds)
    ]
    hbm = pl.BlockSpec(memory_space=pltpu.HBM)
    vmem = pl.BlockSpec(memory_space=pltpu.VMEM)
    dma = pltpu.SemaphoreType.DMA
    shard = jax.ShapeDtypeStruct((96, LANE), F32)
    rows = query_rows + gate_rows
    new_m, new_v, new_s, weights = pl.pallas_call(
        functools.partial(kernel, stop),
        out_shape=(
            pltpu.VMEM(shard.shape, F32), pltpu.VMEM(shard.shape, F32), pltpu.VMEM(shard.shape, F32),
            pltpu.VMEM((2, 2, 3, 4, 4, 4, HALF, LANE), BF16),
        ),
        in_specs=[hbm] * 6,
        out_specs=(vmem, vmem, vmem, vmem),
        scratch_shapes=[
            pltpu.VMEM((2, rows, row_width // 4), BF16),
            pltpu.VMEM((2, rows, row_width // 4), BF16),
            pltpu.VMEM((2, rows, PITCH, LANE), F32),
            pltpu.VMEM((3, 2, 4, 4, 4, HALF, LANE), jnp.int16),
            pltpu.VMEM((3, 2, 3, 4, 4, HALF, LANE), jnp.int16),
            pltpu.VMEM((3, 4, 4, HALF, LANE), F32),
            pltpu.VMEM((3, 2, 16, HALF, LANE), jnp.int16),
            pltpu.VMEM((2, 3, 16, HALF, LANE), jnp.int16),
            pltpu.VMEM((3, 368, LANE), F32),
            pltpu.VMEM((3, 96, LANE), F32),
            pltpu.VMEM((3, 96, LANE), F32),
            pltpu.SMEM((1, 2), jnp.int32),
            dma((4,)),
            pltpu.SemaphoreType.REGULAR((4,)),
            dma((9,)),
            dma((2,)), dma((18,)), dma((6,)),
            dma((6,)), dma((18,)), dma((18,)), dma((1,)), dma((1,)),
        ],
        compiler_params=pltpu.CompilerParams(
            collective_id=0, has_side_effects=True, vmem_limit_bytes=48 * 1024 * 1024
        ),
    )(query, gate, *old, old_bounds)
    query_new, gate_new, new_m, new_v, new_s = pl.pallas_call(
        write,
        out_shape=(
            jax.ShapeDtypeStruct((query_rows, row_width), BF16),
            jax.ShapeDtypeStruct((gate_rows, row_width), BF16),
            shard, shard, shard,
        ),
        in_specs=[vmem] * 4,
        out_specs=(hbm,) * 5,
        scratch_shapes=[pltpu.VMEM((rows, row_width), BF16), dma((rows // 16 + 3,))],
        compiler_params=pltpu.CompilerParams(vmem_limit_bytes=48 * 1024 * 1024),
    )(weights, new_m, new_v, new_s)
    return (new_m.reshape(-1), new_v.reshape(-1), new_s.reshape(-1), query_new, gate_new)


def solution(mesh, stop=9):
    placed = (P("dp", None, None), P("dp", None, None), P("dp"), P("dp"), P("dp"), P("dp", None))
    return jax.shard_map(
        functools.partial(on_device, stop=stop),
        mesh=mesh,
        in_specs=placed,
        out_specs=(P("dp"), P("dp"), P("dp"), P(), P()),
        check_vma=False,
    )
```

```python
import functools

import jax
import jax.numpy as jnp
from jax import lax
from jax.experimental import pallas as pl
from jax.experimental.pallas import tpu as pltpu
from jax.sharding import PartitionSpec as P

MESH = pl.DeviceIdType.MESH
F32 = jnp.float32
BF16 = jnp.bfloat16

STEP = 10
beta_one = 0.9
beta_two = 0.95
learn_rate = 0.01
decay_rate = 0.1
epsilon = 1e-08

LANE = 128
BLK = 32
HALF = 16
PITCH = 24
BOUND = (48.0, 192.0)
AWAY = ((2, 2), (2, 1), (1, 2), (2, -1), (-1, 2), (1, 1), (1, -1), (-1, 1), (-1, -1),
        (2, 0), (0, 2), (1, 0), (0, 1), (-1, 0), (0, -1))
ORDER = ((0, 1, 2), (1, 2, 0), (2, 0, 1))


def adamw_step(master, moment, variance, grad):
    moment_new = beta_one * moment + (1.0 - beta_one) * grad
    variance_new = beta_two * variance + (1.0 - beta_two) * grad * grad
    corrected_m = moment_new / (1.0 - beta_one**STEP)
    corrected_v = variance_new / (1.0 - beta_two**STEP)
    master_new = master - learn_rate * (
        corrected_m / (jnp.sqrt(corrected_v) + epsilon) + decay_rate * master
    )
    return (master_new, moment_new, variance_new)


def encode(value, bound):
    ratio = jnp.maximum(jnp.abs(value), 1e-30) * (1.0 / bound)
    root = lax.rsqrt(lax.rsqrt(ratio))
    code = root * lax.rsqrt(root) * 32767.0
    return jnp.round(jnp.where(value < 0, -code, code)).astype(jnp.int32).astype(jnp.int16)


def decode(code, bound):
    root = code.astype(jnp.int32).astype(F32) * (bound**0.125 / 32767.0)
    square = root * root
    return (root * jnp.abs(root)) * (square * (square * square))


def kernel(
    stop,
    query, gate, old_m, old_v, old_s, bounds_hbm,
    new_m, new_v, new_s, weights,
    mine, other, s0, e0, r0, s1, e1, r1, state, passed, arrived, bounds,
    load_sem, near_sem, send_sem, s0_recv, s1_recv, s2_recv, g1_recv, g3_recv, c_recv, p_recv,
):
    me = lax.axis_index("dp")
    core = me % 2
    chip = me // 2
    at = (chip // 16, (chip // 4) % 4, chip % 4)
    sibling = me + 1 - 2 * core

    def device(moves, on_core):
        place = [(at[axis] + moves.get(axis, 0)) % 4 for axis in range(3)]
        return ((place[0] * 4 + place[1]) * 4 + place[2]) * 2 + on_core

    def remote(src, dst, send, recv, to):
        return pltpu.make_async_remote_copy(
            src_ref=src, dst_ref=dst, send_sem=send, recv_sem=recv,
            device_id=(to,), device_id_type=MESH,
        )

    def start(src, dst, send, recv, to):
        remote(src, dst, send_sem.at[send], recv, to).start()

    def await_from(dst, recv):
        remote(dst, dst, send_sem.at[0], recv, sibling).wait_recv()

    def done():
        totals = (
            other, e0.at[:, :, pl.ds(0, 3)], e1.at[:, :, pl.ds(0, 15)],
            weights.at[0, :, :, 0, 0, pl.ds(0, 3)], weights.at[0, :, :, 0, pl.ds(0, 3)],
            weights.at[0, :, :, pl.ds(0, 3)], weights.at[0],
        )
        for n in range({0: 1, 1: 2, 3: 3}.get(stop, 7)):
            remote(totals[n], totals[n], send_sem.at[n], s0_recv.at[0], sibling).wait_send()
        if stop > 1:
            for p, on_core in ((0, 1), (2, 0)):
                @pl.when(core == on_core)
                def _(p=p):
                    remote(e1.at[p, :, 0], e1.at[p, :, 0], send_sem.at[8], s0_recv.at[0], sibling).wait_send()

        @pl.when(hands_on)
        def _():
            handed.wait_send()

        if 0 <= stop < 3:
            @pl.when(takes)
            def _():
                handed.wait_recv()

    barrier = pltpu.get_barrier_semaphore()
    around = [sibling] + [device({axis: by}, core) for axis in range(3) for by in (1, 3)]

    def greet(sem):
        for to in around:
            pl.semaphore_signal(sem, inc=1, device_id=(to,), device_id_type=MESH)

    greet(barrier)

    wide = mine.shape[2]
    split = query.shape[0]
    loads, olds, swaps = [], [], []
    for g in range(2):
        own_half = pl.ds(pl.multiple_of((2 * core + g) * wide, wide), wide)
        its_half = pl.ds(pl.multiple_of((2 - 2 * core + g) * wide, wide), wide)
        for n, (array, rows) in enumerate(((query, pl.ds(0, split)), (gate, pl.ds(split, gate.shape[0])))):
            loads.append(pltpu.make_async_copy(
                array.at[:, own_half], mine.at[g, rows], load_sem.at[g]))
            swaps.append(remote(
                array.at[:, its_half], other.at[g, rows], send_sem.at[0], s0_recv.at[g], sibling))
    for n, old in enumerate((old_m, old_v, old_s)):
        olds.append(
            pltpu.make_async_copy(old, state.at[n, pl.ds(96, 176)], load_sem.at[2])
        )
    olds.append(pltpu.make_async_copy(bounds_hbm, bounds, load_sem.at[3]))
    for copy in loads + olds:
        copy.start()

    pl.semaphore_wait(barrier, len(around))

    for copy in swaps:
        copy.start()
    greet(near_sem.at[0])

    hands_on = (core == 0) | (at[2] % 2 == 0)
    takes = (core == 1) | (at[2] % 2 == 1)
    handed = remote(
        passed, arrived, send_sem.at[7], p_recv.at[0],
        sibling * (1 - core) + device({2: 1}, 0) * core,
    )

    for n in range(3):
        state[n, pl.ds(0, 96)] = jnp.zeros((96, LANE), F32)
        state[n, pl.ds(272, 96)] = jnp.zeros((96, LANE), F32)
    olds[-1].wait()
    whole = state.at[:, pl.ds(96, 176)]
    pltpu.make_async_copy(whole, whole, load_sem.at[2]).wait()
    first = bounds[0, 0] // LANE
    last = bounds[0, 1] // LANE

    def window(n, base):
        rows = lax.broadcasted_iota(jnp.int32, (96, LANE), 0) + base
        piece = state[n, pl.ds(jnp.clip(base - first + 96, 0, 272), 96)]
        return jnp.where((rows >= first) & (rows < last), piece, 0.0)

    for n in range(3):
        passed[n] = window(n, (me + 1) * 96)
    for n, ref in enumerate((new_m, new_v, new_s)):
        ref[...] = window(n, me * 96)

    def round_of(n):
        pl.semaphore_wait(near_sem.at[n], len(around))
        if n < 3:
            greet(near_sem.at[n + 1])

    flat0 = s0.reshape(2 * 192 * PITCH, LANE)
    blocks0 = s0.reshape(2, 4, 4, 4, 3, PITCH, LANE)
    rows0 = pl.ds(0, HALF)

    def block(p, g, a, b, c):
        place = [None] * 3
        for axis, value in zip(ORDER[p], (a, b, c)):
            place[axis] = value
        return blocks0[g, place[0], place[1], place[2], p, rows0]

    def slab_out(p, g, by):
        a = (at[ORDER[p][0]] + by) % 4

        def code(b, carry):
            for c in range(4):
                e0[p, g, a, b, c] = encode(block(p, g, a, b, c), BOUND[0])
            return carry

        lax.fori_loop(0, 4, code, 0)
        start(
            e0.at[p, g, a], r0.at[p, g, by - 1], 1, s1_recv.at[(p * 2 + g) * 3 + by - 1],
            device({ORDER[p][0]: by}, core),
        )

    for g in range(2):
        pltpu.make_async_copy(mine.at[g], mine.at[g], load_sem.at[g]).wait()
        await_from(other.at[g], s0_recv.at[g])

        def pair(i, carry, g=g):
            row = pl.multiple_of(16 * i, 16)
            for j in range(HALF):
                lanes = pl.ds(j * LANE, LANE)
                both = mine[g, pl.ds(row, 16), lanes].astype(F32) + other[g, pl.ds(row, 16), lanes].astype(F32)
                flat0[pl.ds((g * 192 + row) * PITCH + j, 16, stride=PITCH), :] = both
            return carry

        lax.fori_loop(0, 12, pair, 0)
        for by in (1, 3, 2):
            if by == 2:
                round_of(g)
            for p in range(3):
                if stop != 0:
                    slab_out(p, g, by)
        if g == 0:
            @pl.when(hands_on)
            def _():
                handed.start()
    round_of(2)
    if stop == 0:
        round_of(3)
        return done()

    def plane_out(g):
        for p in range(3):
            for by in (1, 3):
                await_from(r0.at[p, g, by - 1], s1_recv.at[(p * 2 + g) * 3 + by - 1])

            def gather_one(b, carry, p=p):
                for c in range(4):
                    s1[p, b, c] = block(p, g, at[ORDER[p][0]], b, c) + (
                        decode(r0[p, g, 0, b, c], BOUND[0]) + decode(r0[p, g, 2, b, c], BOUND[0]))
                return carry

            lax.fori_loop(0, 4, gather_one, 0)
        if g == 0:
            round_of(3)
        for p in range(3):
            await_from(r0.at[p, g, 1], s1_recv.at[(p * 2 + g) * 3 + 1])

            def gather_two(b, carry, p=p):
                for c in range(4):
                    total = s1[p, b, c] + decode(r0[p, g, 1, b, c], BOUND[0])
                    e1[p, g, b * 4 + c] = encode(total, BOUND[1])
                return carry

            lax.fori_loop(0, 4, gather_two, 0)
            if stop == 1:
                continue
            _, b, c = ORDER[p]
            unit = 2 * p + core
            owner = unit // 3
            place = unit % 3
            source = at[b] * 4 + at[c]
            for db, dc in AWAY:
                start(
                    e1.at[p, g, (at[b] + db) % 4 * 4 + (at[c] + dc) % 4], r1.at[g, place, source],
                    2, s2_recv.at[g * 3 + place], device({b: db, c: dc}, owner),
                )
            if p == 1:
                r1[g, place, source] = e1[p, g, source]
            else:
                crosses = core == (1 if p == 0 else 0)

                @pl.when(crosses)
                def _(p=p, place=place, source=source):
                    start(
                        e1.at[p, g, source], r1.at[g, place, source],
                        8, s2_recv.at[g * 3 + place], sibling,
                    )

                @pl.when(jnp.logical_not(crosses))
                def _(p=p, place=place, source=source):
                    r1[g, place, source] = e1[p, g, source]

    def group(m, g, da, db):
        a, b, _ = ORDER[m]
        return weights.at[core, g, m, (at[a] + da) % 4, (at[b] + db) % 4]

    def step(g):
        for m in range(3):
            await_from(r1.at[g, m, pl.ds(0, 16 if m == 1 else 15)], s2_recv.at[g * 3 + m])
            values = [decode(r1[g, m, n], BOUND[1]) for n in range(16)]
            while len(values) > 1:
                values = [one + two for one, two in zip(values[::2], values[1::2])]
            rows = pl.ds(m * BLK + g * HALF, HALF)
            master, moment, variance = adamw_step(new_m[rows], new_v[rows], new_s[rows], values[0])
            new_m[rows] = master
            new_v[rows] = moment
            new_s[rows] = variance
            own = weights.at[(core, g, m) + tuple(at[axis] for axis in ORDER[m])]
            own[...] = master.astype(BF16)
            if stop == 3:
                continue
            for db, dc in AWAY:
                start(
                    own, own, 4 if db else 3, g1_recv.at[(g * 3 + m) * 4 + db % 4],
                    device({ORDER[m][1]: db, ORDER[m][2]: dc}, core),
                )

    def group_out(m, g, db):
        part = group(m, g, 0, -db)
        for by in (2, 1, 3):
            start(part, part, 5, g3_recv.at[(g * 3 + m) * 3 + by - 1], device({ORDER[m][0]: by}, core))

    def near_group(g):
        for m in range(3):
            await_from(weights.at[0, g, m, 0, 0, pl.ds(0, 3)], g1_recv.at[(g * 3 + m) * 4])
            group_out(m, g, 0)

    def other_groups(g):
        for by in (1, 3, 2):
            for m in range(3):
                await_from(group(m, g, 0, -by), g1_recv.at[(g * 3 + m) * 4 + by])
                group_out(m, g, by)

    def forward(g):
        for by in (0, 1, 3, 2):
            for m in range(3):
                part = weights.at[core, g, m, (at[ORDER[m][0]] - by) % 4]
                if by:
                    await_from(part, g3_recv.at[(g * 3 + m) * 3 + by - 1])
                start(part, part, 6, c_recv.at[0], sibling)

    for g in range(2):
        plane_out(g)
    if stop == 1:
        return done()

    @pl.when(takes)
    def _():
        handed.wait_recv()

    @pl.when(jnp.logical_not(takes))
    def _():
        arrived[...] = jnp.zeros_like(arrived)

    for n, ref in enumerate((new_m, new_v, new_s)):
        ref[...] += arrived[n]

    step(0)
    step(1)
    if stop == 3:
        return done()
    near_group(0)
    other_groups(0)
    near_group(1)
    other_groups(1)
    forward(0)
    forward(1)
    await_from(weights.at[0], c_recv.at[0])
    done()


def write(weights, new_m, new_v, new_s, query, gate, out_m, out_v, out_s, tiles, sems):
    split, rows = query.shape[0], tiles.shape[0]
    copies = [
        pltpu.make_async_copy(src, dst, sems.at[rows // 16 + n])
        for n, (src, dst) in enumerate(((new_m, out_m), (new_v, out_v), (new_s, out_s)))
    ]

    def rows_of(x, third):
        i = 3 * x + third
        at = pl.ds(pl.multiple_of(16 * i, 16), 16)
        for j in range(0, 2 * BLK, 8):
            picked = []
            for row in range(16 * third, 16 * third + 16):
                chip = (x, row // 12, row // 3 % 4)
                unit = row % 3 * 2 + j // BLK
                m = unit % 3
                place = (unit // 3, j % BLK // HALF, m) + tuple(chip[axis] for axis in ORDER[m])
                picked.append(weights[place + (pl.ds(j % HALF, 8),)])
            block = jnp.swapaxes(jnp.stack(picked), 0, 1)
            for k in range(8):
                tiles[at, pl.ds((j + k) * LANE, LANE)] = block[k]

        @pl.when(i < split // 16)
        def _():
            pltpu.make_async_copy(tiles.at[at], query.at[at], sems.at[i]).start()

        @pl.when(i >= split // 16)
        def _():
            to = pl.ds(pl.multiple_of(16 * i - split, 16), 16)
            pltpu.make_async_copy(tiles.at[at], gate.at[to], sems.at[i]).start()

    def plane(x, carry):
        for third in range(3):
            rows_of(x, third)
        return carry

    for copy in copies:
        copy.start()
    lax.fori_loop(0, 4, plane, 0)
    for i in range(rows // 16):
        to = query.at[pl.ds(16 * i, 16)] if 16 * i < split else gate.at[pl.ds(16 * i - split, 16)]
        copies.append(pltpu.make_async_copy(tiles.at[pl.ds(16 * i, 16)], to, sems.at[i]))
    for copy in copies:
        copy.wait()


def on_device(grad_query, grad_gate, old_master, old_moment, old_variance, old_bounds, stop=9):
    query_rows, row_width = grad_query.shape[1:]
    gate_rows = grad_gate.shape[1]
    query = grad_query.reshape(query_rows, row_width)
    gate = grad_gate.reshape(gate_rows, row_width)
    old = [a.reshape(-1, LANE) for a in (old_master, old_moment, old_variance)]
    query, gate, *old, old_bounds = [
        pltpu.with_memory_space_constraint(a, pltpu.HBM) for a in (query, gate, *old, old_bounds)
    ]
    hbm = pl.BlockSpec(memory_space=pltpu.HBM)
    vmem = pl.BlockSpec(memory_space=pltpu.VMEM)
    dma = pltpu.SemaphoreType.DMA
    shard = jax.ShapeDtypeStruct((96, LANE), F32)
    rows = query_rows + gate_rows
    new_m, new_v, new_s, weights = pl.pallas_call(
        functools.partial(kernel, stop),
        out_shape=(
            pltpu.VMEM(shard.shape, F32), pltpu.VMEM(shard.shape, F32), pltpu.VMEM(shard.shape, F32),
            pltpu.VMEM((2, 2, 3, 4, 4, 4, HALF, LANE), BF16),
        ),
        in_specs=[hbm] * 6,
        out_specs=(vmem, vmem, vmem, vmem),
        scratch_shapes=[
            pltpu.VMEM((2, rows, row_width // 4), BF16),
            pltpu.VMEM((2, rows, row_width // 4), BF16),
            pltpu.VMEM((2, rows, PITCH, LANE), F32),
            pltpu.VMEM((3, 2, 4, 4, 4, HALF, LANE), jnp.int16),
            pltpu.VMEM((3, 2, 3, 4, 4, HALF, LANE), jnp.int16),
            pltpu.VMEM((3, 4, 4, HALF, LANE), F32),
            pltpu.VMEM((3, 2, 16, HALF, LANE), jnp.int16),
            pltpu.VMEM((2, 3, 16, HALF, LANE), jnp.int16),
            pltpu.VMEM((3, 368, LANE), F32),
            pltpu.VMEM((3, 96, LANE), F32),
            pltpu.VMEM((3, 96, LANE), F32),
            pltpu.SMEM((1, 2), jnp.int32),
            dma((4,)),
            pltpu.SemaphoreType.REGULAR((4,)),
            dma((9,)),
            dma((2,)), dma((18,)), dma((6,)),
            dma((24,)), dma((18,)), dma((1,)), dma((1,)),
        ],
        compiler_params=pltpu.CompilerParams(
            collective_id=0, has_side_effects=True, vmem_limit_bytes=48 * 1024 * 1024
        ),
    )(query, gate, *old, old_bounds)
    query_new, gate_new, new_m, new_v, new_s = pl.pallas_call(
        write,
        out_shape=(
            jax.ShapeDtypeStruct((query_rows, row_width), BF16),
            jax.ShapeDtypeStruct((gate_rows, row_width), BF16),
            shard, shard, shard,
        ),
        in_specs=[vmem] * 4,
        out_specs=(hbm,) * 5,
        scratch_shapes=[pltpu.VMEM((rows, row_width), BF16), dma((rows // 16 + 3,))],
        compiler_params=pltpu.CompilerParams(vmem_limit_bytes=48 * 1024 * 1024),
    )(weights, new_m, new_v, new_s)
    return (new_m.reshape(-1), new_v.reshape(-1), new_s.reshape(-1), query_new, gate_new)


def solution(mesh, stop=9):
    placed = (P("dp", None, None), P("dp", None, None), P("dp"), P("dp"), P("dp"), P("dp", None))
    return jax.shard_map(
        functools.partial(on_device, stop=stop),
        mesh=mesh,
        in_specs=placed,
        out_specs=(P("dp"), P("dp"), P("dp"), P(), P()),
        check_vma=False,
    )
```

```python
import functools

import jax
import jax.numpy as jnp
from jax import lax
from jax.experimental import pallas as pl
from jax.experimental.pallas import tpu as pltpu
from jax.sharding import PartitionSpec as P

MESH = pl.DeviceIdType.MESH
F32 = jnp.float32
BF16 = jnp.bfloat16

STEP = 10
beta_one = 0.9
beta_two = 0.95
learn_rate = 0.01
decay_rate = 0.1
epsilon = 1e-08

LANE = 128
BLK = 32
HALF = 16
PITCH = 24
BOUND = (48.0, 192.0)
AWAY = ((2, 2), (2, 1), (1, 2), (2, -1), (-1, 2), (1, 1), (1, -1), (-1, 1), (-1, -1),
        (2, 0), (0, 2), (1, 0), (0, 1), (-1, 0), (0, -1))
ORDER = ((0, 1, 2), (1, 2, 0), (2, 0, 1))


def adamw_step(master, moment, variance, grad):
    moment_new = beta_one * moment + (1.0 - beta_one) * grad
    variance_new = beta_two * variance + (1.0 - beta_two) * grad * grad
    corrected_m = moment_new / (1.0 - beta_one**STEP)
    corrected_v = variance_new / (1.0 - beta_two**STEP)
    master_new = master - learn_rate * (
        corrected_m / (jnp.sqrt(corrected_v) + epsilon) + decay_rate * master
    )
    return (master_new, moment_new, variance_new)


def encode(value, bound):
    ratio = jnp.maximum(jnp.abs(value), 1e-30) * (1.0 / bound)
    root = lax.rsqrt(lax.rsqrt(ratio))
    code = root * lax.rsqrt(root) * 32767.0
    return jnp.round(jnp.where(value < 0, -code, code)).astype(jnp.int32).astype(jnp.int16)


def decode(code, bound):
    root = code.astype(jnp.int32).astype(F32) * (bound**0.125 / 32767.0)
    square = root * root
    return (root * jnp.abs(root)) * (square * (square * square))


def kernel(
    stop,
    query, gate, old_m, old_v, old_s, bounds_hbm,
    new_m, new_v, new_s, weights,
    mine, other, s0, e0, r0, s1, e1, r1, state, passed, arrived, bounds,
    load_sem, near_sem, send_sem, s0_recv, s1_recv, s2_recv, g1_recv, g3_recv, c_recv, p_recv,
):
    me = lax.axis_index("dp")
    core = me % 2
    chip = me // 2
    at = (chip // 16, (chip // 4) % 4, chip % 4)
    sibling = me + 1 - 2 * core

    def device(moves, on_core):
        place = [(at[axis] + moves.get(axis, 0)) % 4 for axis in range(3)]
        return ((place[0] * 4 + place[1]) * 4 + place[2]) * 2 + on_core

    def remote(src, dst, send, recv, to):
        return pltpu.make_async_remote_copy(
            src_ref=src, dst_ref=dst, send_sem=send, recv_sem=recv,
            device_id=(to,), device_id_type=MESH,
        )

    def start(src, dst, send, recv, to):
        remote(src, dst, send_sem.at[send], recv, to).start()

    def await_from(dst, recv):
        remote(dst, dst, send_sem.at[0], recv, sibling).wait_recv()

    def done():
        totals = (
            other, e0.at[:, :, pl.ds(0, 3)], e1.at[:, :, pl.ds(0, 15)],
            weights.at[0, :, :, 0, 0, pl.ds(0, 3)], weights.at[0, :, :, 0, pl.ds(0, 3)],
            weights.at[0, :, :, pl.ds(0, 3)], weights.at[0],
        )
        for n in range({0: 1, 1: 2, 3: 3}.get(stop, 7)):
            remote(totals[n], totals[n], send_sem.at[n], s0_recv.at[0], sibling).wait_send()
        if stop > 1:
            for p, on_core in ((0, 1), (2, 0)):
                @pl.when(core == on_core)
                def _(p=p):
                    remote(e1.at[p, :, 0], e1.at[p, :, 0], send_sem.at[8], s0_recv.at[0], sibling).wait_send()

        @pl.when(hands_on)
        def _():
            handed.wait_send()

        if 0 <= stop < 3:
            @pl.when(takes)
            def _():
                handed.wait_recv()

    barrier = pltpu.get_barrier_semaphore()
    around = [sibling] + [device({axis: by}, core) for axis in range(3) for by in (1, 3)]

    def greet(sem):
        for to in around:
            pl.semaphore_signal(sem, inc=1, device_id=(to,), device_id_type=MESH)

    greet(barrier)

    wide = mine.shape[2]
    split = query.shape[0]
    loads, olds, swaps = [], [], []
    for g in range(2):
        own_half = pl.ds(pl.multiple_of((2 * core + g) * wide, wide), wide)
        its_half = pl.ds(pl.multiple_of((2 - 2 * core + g) * wide, wide), wide)
        for n, (array, rows) in enumerate(((query, pl.ds(0, split)), (gate, pl.ds(split, gate.shape[0])))):
            loads.append(pltpu.make_async_copy(
                array.at[:, own_half], mine.at[g, rows], load_sem.at[g]))
            swaps.append(remote(
                array.at[:, its_half], other.at[g, rows], send_sem.at[0], s0_recv.at[g], sibling))
    for n, old in enumerate((old_m, old_v, old_s)):
        olds.append(
            pltpu.make_async_copy(old, state.at[n, pl.ds(96, 176)], load_sem.at[2])
        )
    olds.append(pltpu.make_async_copy(bounds_hbm, bounds, load_sem.at[3]))
    for copy in loads + olds:
        copy.start()

    pl.semaphore_wait(barrier, len(around))

    for copy in swaps:
        copy.start()
    greet(near_sem.at[0])

    hands_on = (core == 0) | (at[2] % 2 == 0)
    takes = (core == 1) | (at[2] % 2 == 1)
    handed = remote(
        passed, arrived, send_sem.at[7], p_recv.at[0],
        sibling * (1 - core) + device({2: 1}, 0) * core,
    )

    for n in range(3):
        state[n, pl.ds(0, 96)] = jnp.zeros((96, LANE), F32)
        state[n, pl.ds(272, 96)] = jnp.zeros((96, LANE), F32)
    olds[-1].wait()
    whole = state.at[:, pl.ds(96, 176)]
    pltpu.make_async_copy(whole, whole, load_sem.at[2]).wait()
    first = bounds[0, 0] // LANE
    last = bounds[0, 1] // LANE

    def window(n, base):
        rows = lax.broadcasted_iota(jnp.int32, (96, LANE), 0) + base
        piece = state[n, pl.ds(jnp.clip(base - first + 96, 0, 272), 96)]
        return jnp.where((rows >= first) & (rows < last), piece, 0.0)

    for n in range(3):
        passed[n] = window(n, (me + 1) * 96)
    for n, ref in enumerate((new_m, new_v, new_s)):
        ref[...] = window(n, me * 96)

    def round_of(n):
        pl.semaphore_wait(near_sem.at[n], len(around))
        if n < 3:
            greet(near_sem.at[n + 1])

    flat0 = s0.reshape(2 * 192 * PITCH, LANE)
    blocks0 = s0.reshape(2, 4, 4, 4, 3, PITCH, LANE)
    rows0 = pl.ds(0, HALF)

    def block(p, g, a, b, c):
        place = [None] * 3
        for axis, value in zip(ORDER[p], (a, b, c)):
            place[axis] = value
        return blocks0[g, place[0], place[1], place[2], p, rows0]

    def slab_out(p, g, by):
        a = (at[ORDER[p][0]] + by) % 4

        def code(b, carry):
            for c in range(4):
                e0[p, g, a, b, c] = encode(block(p, g, a, b, c), BOUND[0])
            return carry

        lax.fori_loop(0, 4, code, 0, unroll=2)
        start(
            e0.at[p, g, a], r0.at[p, g, by - 1], 1, s1_recv.at[(p * 2 + g) * 2 + int(by == 2)],
            device({ORDER[p][0]: by}, core),
        )

    for g in range(2):
        pltpu.make_async_copy(mine.at[g], mine.at[g], load_sem.at[g]).wait()
        await_from(other.at[g], s0_recv.at[g])

        def pair(i, carry, g=g):
            row = pl.multiple_of(16 * i, 16)
            for j in range(HALF):
                lanes = pl.ds(j * LANE, LANE)
                both = mine[g, pl.ds(row, 16), lanes].astype(F32) + other[g, pl.ds(row, 16), lanes].astype(F32)
                flat0[pl.ds((g * 192 + row) * PITCH + j, 16, stride=PITCH), :] = both
            return carry

        lax.fori_loop(0, 12, pair, 0)
        for by in (1, 3, 2):
            if by == 2:
                round_of(g)
            for p in range(3):
                if stop != 0:
                    slab_out(p, g, by)
        if g == 0:
            @pl.when(hands_on)
            def _():
                handed.start()
    round_of(2)
    if stop == 0:
        round_of(3)
        return done()

    def plane_out(g):
        for p in range(3):
            await_from(r0.at[p, g, pl.ds(0, 2)], s1_recv.at[(p * 2 + g) * 2])

            def gather_one(b, carry, p=p):
                for c in range(4):
                    s1[p, b, c] = block(p, g, at[ORDER[p][0]], b, c) + (
                        decode(r0[p, g, 0, b, c], BOUND[0]) + decode(r0[p, g, 2, b, c], BOUND[0]))
                return carry

            lax.fori_loop(0, 4, gather_one, 0, unroll=2)
        if g == 0:
            round_of(3)
        for p in range(3):
            await_from(r0.at[p, g, 1], s1_recv.at[(p * 2 + g) * 2 + 1])

            def gather_two(b, carry, p=p):
                for c in range(4):
                    total = s1[p, b, c] + decode(r0[p, g, 1, b, c], BOUND[0])
                    e1[p, g, b * 4 + c] = encode(total, BOUND[1])
                return carry

            lax.fori_loop(0, 4, gather_two, 0, unroll=2)
            if stop == 1:
                continue
            _, b, c = ORDER[p]
            unit = 2 * p + core
            owner = unit // 3
            place = unit % 3
            source = at[b] * 4 + at[c]
            for db, dc in AWAY:
                start(
                    e1.at[p, g, (at[b] + db) % 4 * 4 + (at[c] + dc) % 4], r1.at[g, place, source],
                    2, s2_recv.at[g * 3 + place], device({b: db, c: dc}, owner),
                )
            if p == 1:
                r1[g, place, source] = e1[p, g, source]
            else:
                crosses = core == (1 if p == 0 else 0)

                @pl.when(crosses)
                def _(p=p, place=place, source=source):
                    start(
                        e1.at[p, g, source], r1.at[g, place, source],
                        8, s2_recv.at[g * 3 + place], sibling,
                    )

                @pl.when(jnp.logical_not(crosses))
                def _(p=p, place=place, source=source):
                    r1[g, place, source] = e1[p, g, source]

    def group(m, g, da, db):
        a, b, _ = ORDER[m]
        return weights.at[core, g, m, (at[a] + da) % 4, (at[b] + db) % 4]

    def step(g):
        for m in range(3):
            await_from(r1.at[g, m, pl.ds(0, 16 if m == 1 else 15)], s2_recv.at[g * 3 + m])
            values = [decode(r1[g, m, n], BOUND[1]) for n in range(16)]
            while len(values) > 1:
                values = [one + two for one, two in zip(values[::2], values[1::2])]
            rows = pl.ds(m * BLK + g * HALF, HALF)
            master, moment, variance = adamw_step(new_m[rows], new_v[rows], new_s[rows], values[0])
            new_m[rows] = master
            new_v[rows] = moment
            new_s[rows] = variance
            own = weights.at[(core, g, m) + tuple(at[axis] for axis in ORDER[m])]
            own[...] = master.astype(BF16)
            if stop == 3:
                continue
            for db, dc in AWAY:
                start(
                    own, own, 4 if db else 3, g1_recv.at[(g * 3 + m) * 4 + db % 4],
                    device({ORDER[m][1]: db, ORDER[m][2]: dc}, core),
                )

    def group_out(m, g, db):
        part = group(m, g, 0, -db)
        for by in (1, 3, 2):
            start(part, part, 5, g3_recv.at[(g * 3 + m) * 3 + by - 1], device({ORDER[m][0]: by}, core))

    def near_group(g):
        for m in range(3):
            await_from(weights.at[0, g, m, 0, 0, pl.ds(0, 3)], g1_recv.at[(g * 3 + m) * 4])
            group_out(m, g, 0)

    def other_groups(g):
        for m in range(3):
            for by in (1, 3, 2):
                await_from(group(m, g, 0, -by), g1_recv.at[(g * 3 + m) * 4 + by])
                group_out(m, g, by)

    def forward(g):
        for by in (0, 1, 3, 2):
            for m in range(3):
                part = weights.at[core, g, m, (at[ORDER[m][0]] - by) % 4]
                if by:
                    await_from(part, g3_recv.at[(g * 3 + m) * 3 + by - 1])
                start(part, part, 6, c_recv.at[0], sibling)

    for g in range(2):
        plane_out(g)
    if stop == 1:
        return done()

    @pl.when(takes)
    def _():
        handed.wait_recv()

    @pl.when(jnp.logical_not(takes))
    def _():
        arrived[...] = jnp.zeros_like(arrived)

    for n, ref in enumerate((new_m, new_v, new_s)):
        ref[...] += arrived[n]

    step(0)
    step(1)
    if stop == 3:
        return done()
    near_group(0)
    other_groups(0)
    near_group(1)
    other_groups(1)
    forward(0)
    forward(1)
    await_from(weights.at[0], c_recv.at[0])
    done()


def write(weights, new_m, new_v, new_s, query, gate, out_m, out_v, out_s, tiles, sems):
    split, rows = query.shape[0], tiles.shape[0]
    copies = [
        pltpu.make_async_copy(src, dst, sems.at[rows // 16 + n])
        for n, (src, dst) in enumerate(((new_m, out_m), (new_v, out_v), (new_s, out_s)))
    ]

    def rows_of(x, third):
        i = 3 * x + third
        at = pl.ds(pl.multiple_of(16 * i, 16), 16)
        for j in range(0, 2 * BLK, 8):
            picked = []
            for row in range(16 * third, 16 * third + 16):
                chip = (x, row // 12, row // 3 % 4)
                unit = row % 3 * 2 + j // BLK
                m = unit % 3
                place = (unit // 3, j % BLK // HALF, m) + tuple(chip[axis] for axis in ORDER[m])
                picked.append(weights[place + (pl.ds(j % HALF, 8),)])
            block = jnp.swapaxes(jnp.stack(picked), 0, 1)
            for k in range(8):
                tiles[at, pl.ds((j + k) * LANE, LANE)] = block[k]

        @pl.when(i < split // 16)
        def _():
            pltpu.make_async_copy(tiles.at[at], query.at[at], sems.at[i]).start()

        @pl.when(i >= split // 16)
        def _():
            to = pl.ds(pl.multiple_of(16 * i - split, 16), 16)
            pltpu.make_async_copy(tiles.at[at], gate.at[to], sems.at[i]).start()

    def plane(x, carry):
        for third in range(3):
            rows_of(x, third)
        return carry

    for copy in copies:
        copy.start()
    lax.fori_loop(0, 4, plane, 0)
    for i in range(rows // 16):
        to = query.at[pl.ds(16 * i, 16)] if 16 * i < split else gate.at[pl.ds(16 * i - split, 16)]
        copies.append(pltpu.make_async_copy(tiles.at[pl.ds(16 * i, 16)], to, sems.at[i]))
    for copy in copies:
        copy.wait()


def on_device(grad_query, grad_gate, old_master, old_moment, old_variance, old_bounds, stop=9):
    query_rows, row_width = grad_query.shape[1:]
    gate_rows = grad_gate.shape[1]
    query = grad_query.reshape(query_rows, row_width)
    gate = grad_gate.reshape(gate_rows, row_width)
    old = [a.reshape(-1, LANE) for a in (old_master, old_moment, old_variance)]
    query, gate, *old, old_bounds = [
        pltpu.with_memory_space_constraint(a, pltpu.HBM) for a in (query, gate, *old, old_bounds)
    ]
    hbm = pl.BlockSpec(memory_space=pltpu.HBM)
    vmem = pl.BlockSpec(memory_space=pltpu.VMEM)
    dma = pltpu.SemaphoreType.DMA
    shard = jax.ShapeDtypeStruct((96, LANE), F32)
    rows = query_rows + gate_rows
    new_m, new_v, new_s, weights = pl.pallas_call(
        functools.partial(kernel, stop),
        out_shape=(
            pltpu.VMEM(shard.shape, F32), pltpu.VMEM(shard.shape, F32), pltpu.VMEM(shard.shape, F32),
            pltpu.VMEM((2, 2, 3, 4, 4, 4, HALF, LANE), BF16),
        ),
        in_specs=[hbm] * 6,
        out_specs=(vmem, vmem, vmem, vmem),
        scratch_shapes=[
            pltpu.VMEM((2, rows, row_width // 4), BF16),
            pltpu.VMEM((2, rows, row_width // 4), BF16),
            pltpu.VMEM((2, rows, PITCH, LANE), F32),
            pltpu.VMEM((3, 2, 4, 4, 4, HALF, LANE), jnp.int16),
            pltpu.VMEM((3, 2, 3, 4, 4, HALF, LANE), jnp.int16),
            pltpu.VMEM((3, 4, 4, HALF, LANE), F32),
            pltpu.VMEM((3, 2, 16, HALF, LANE), jnp.int16),
            pltpu.VMEM((2, 3, 16, HALF, LANE), jnp.int16),
            pltpu.VMEM((3, 368, LANE), F32),
            pltpu.VMEM((3, 96, LANE), F32),
            pltpu.VMEM((3, 96, LANE), F32),
            pltpu.SMEM((1, 2), jnp.int32),
            dma((4,)),
            pltpu.SemaphoreType.REGULAR((4,)),
            dma((9,)),
            dma((2,)), dma((12,)), dma((6,)),
            dma((24,)), dma((18,)), dma((1,)), dma((1,)),
        ],
        compiler_params=pltpu.CompilerParams(
            collective_id=0, has_side_effects=True, vmem_limit_bytes=48 * 1024 * 1024
        ),
    )(query, gate, *old, old_bounds)
    query_new, gate_new, new_m, new_v, new_s = pl.pallas_call(
        write,
        out_shape=(
            jax.ShapeDtypeStruct((query_rows, row_width), BF16),
            jax.ShapeDtypeStruct((gate_rows, row_width), BF16),
            shard, shard, shard,
        ),
        in_specs=[vmem] * 4,
        out_specs=(hbm,) * 5,
        scratch_shapes=[pltpu.VMEM((rows, row_width), BF16), dma((rows // 16 + 3,))],
        compiler_params=pltpu.CompilerParams(vmem_limit_bytes=48 * 1024 * 1024),
    )(weights, new_m, new_v, new_s)
    return (new_m.reshape(-1), new_v.reshape(-1), new_s.reshape(-1), query_new, gate_new)


def solution(mesh, stop=9):
    placed = (P("dp", None, None), P("dp", None, None), P("dp"), P("dp"), P("dp"), P("dp", None))
    return jax.shard_map(
        functools.partial(on_device, stop=stop),
        mesh=mesh,
        in_specs=placed,
        out_specs=(P("dp"), P("dp"), P("dp"), P(), P()),
        check_vma=False,
    )
```
